128 devices in a mesh: grp: 16 (over x, z), tp: 8 (over y, core).
Axes of the slice: x: 4, y: 4, z: 4, core: 2. Of those that a mesh axis runs over, the one named last changes fastest.
Arguments:
- actor_rows: bfloat16 [768, 12288], P('grp', 'tp'), may hold values from -6 to 6
- route_counts: int32 [16, 16], replicated, may hold values from 0 to 6, as said below
- targets: int32 [768], replicated, may hold values from 0 to 16383
- pair_index: int32 [128, 2], P(('grp', 'tp')), may hold values from 0 to 255, as said below
- attn_gain: float32 [12288], P('tp'), may hold values from 0.25 to 1.75
- w_query: bfloat16 [12288, 12288], P('tp', 'grp'), may hold values from -0.0546875 to 0.0546875
- key_weight: bfloat16 [12288, 1024], P('tp'), may hold values from -0.0546875 to 0.0546875
- value_weight: bfloat16 [12288, 1024], P('tp'), may hold values from -0.0546875 to 0.0546875
- w_out: bfloat16 [12288, 12288], P('grp', 'tp'), may hold values from -0.0546875 to 0.0546875
- mlp_gain: float32 [12288], P('tp'), may hold values from 0.25 to 1.75
- w_gate: bfloat16 [12288, 14336], P('tp', 'grp'), may hold values from -0.0546875 to 0.0546875
- w_up: bfloat16 [12288, 14336], P('tp', 'grp'), may hold values from -0.0546875 to 0.0546875
- w_down: bfloat16 [14336, 12288], P('grp', 'tp'), may hold values from -0.046875 to 0.046875
- final_gain: float32 [12288], P('tp'), may hold values from 0.25 to 1.75
- w_vocab: bfloat16 [12288, 16384], P('tp', 'grp'), may hold values from -0.15625 to 0.15625
Outputs:
- final_rows: bfloat16 [768, 12288], P('grp', 'tp')
- pair_scores: float32 [128, 12], P(('grp', 'tp'))
The draws below stay inside these ranges and needn't reach their ends.
Inputs may be any that keep to these rules, and one draw needn't show every extreme that they name: route_counts[a, g] rows go from actor group a to reference group g; every row and every column of the table sums to 48; its largest entry equals 6. `pair_index`: each sequence id appears exactly once; id a * 16 + g is the piece sent from actor group a to reference group g, which may be empty.
All inputs are finite; a program needn't handle non-finite values.
Results may differ from the reference program's by a relative error of at most 0.025.
Values may be sent and summed in bfloat16 or wider, within the bound.
No kernel may reach another device: no remote copies, remote signals or barrier semaphores. Data moves between devices by JAX's collectives and lax.ppermute only.
A program may use at most 128 MiB of HBM per device.

```python
import math
import jax
import jax.numpy as jnp
import numpy as np
from jax import lax

MODEL_WIDTH = 12288
QUERY_HEADS = 96
KEY_VALUE_HEADS = 8
HEAD_SIZE = 128
FF = 14336
VOCAB = 16384
ROWS = 48
GROUPS = 16
TOKEN_ROWS = 768
CAP = 6
N_GRP = 16
N_TP = 8


def draw_route_counts(key, part):
    key = jax.random.fold_in(key, 11)
    first_key, second_key, third_key, move_key, row_key, col_key = jax.random.split(key, 6)
    mean_load = ROWS // N_GRP
    cap_size = 2 * mean_load
    shifts = jax.random.randint(first_key, (N_GRP,), 0, mean_load + 1)
    peak_slot = jax.random.randint(second_key, (), 0, N_GRP)
    places = jnp.arange(N_GRP)
    shifts = jnp.where(places == peak_slot, mean_load, shifts)
    shifts = jnp.where(places == (peak_slot + 1) % N_GRP, 0, shifts)
    profile = mean_load + shifts - jnp.roll(shifts, -1)
    offset = jax.random.randint(third_key, (), 0, N_GRP)
    counts_table = profile[(places[None, :] - places[:, None] + offset) % N_GRP].astype(jnp.int32)
    kept_col = (peak_slot - offset) % N_GRP
    move_keys = jax.random.split(move_key, 4 * N_GRP)

    def one_move(step, current):
        sub_keys = jax.random.split(move_keys[step], 5)
        first_row = 1 + jax.random.randint(sub_keys[0], (), 0, N_GRP - 1)
        second_row = 1 + (first_row + jax.random.randint(sub_keys[1], (), 0, N_GRP - 2)) % (N_GRP - 1)
        first_pick = jax.random.randint(sub_keys[2], (), 0, N_GRP - 1)
        second_pick = (first_pick + 1 + jax.random.randint(sub_keys[3], (), 0, N_GRP - 2)) % (N_GRP - 1)
        first_col = (kept_col + 1 + first_pick) % N_GRP
        second_col = (kept_col + 1 + second_pick) % N_GRP
        corner_one = current[first_row, first_col]
        corner_two = current[second_row, second_col]
        corner_three = current[first_row, second_col]
        corner_four = current[second_row, first_col]
        upper = jnp.minimum(jnp.minimum(cap_size - corner_one, cap_size - corner_two), jnp.minimum(corner_three, corner_four))
        lower = -jnp.minimum(jnp.minimum(corner_one, corner_two), jnp.minimum(cap_size - corner_three, cap_size - corner_four))
        amount = jax.random.randint(sub_keys[4], (), lower, upper + 1).astype(jnp.int32)
        current = current.at[first_row, first_col].add(amount)
        current = current.at[second_row, second_col].add(amount)
        current = current.at[first_row, second_col].add(-amount)
        current = current.at[second_row, first_col].add(-amount)
        return current
    counts_table = lax.fori_loop(0, 4 * N_GRP, one_move, counts_table)
    row_order = jax.random.permutation(row_key, N_GRP)
    col_order = jax.random.permutation(col_key, N_GRP)
    counts_table = counts_table[row_order][:, col_order]
    return counts_table.astype(jnp.int32)


def draw_pair_index(key, part):
    key = jax.random.fold_in(key, 23)
    shuffled = jax.random.permutation(key, N_GRP * N_GRP)
    return shuffled.reshape(N_GRP * N_GRP // 2, 2).astype(jnp.int32)


def with_ends(result, rng, low, largest):
    spot = [jax.random.randint(jax.random.fold_in(rng, axis), (), 0, length) for axis, length in enumerate(result.shape)]
    longest = result.shape.index(max(result.shape))
    neighbour = spot[:longest] + [(spot[longest] + 1) % result.shape[longest]] + spot[longest + 1:]
    return result.at[tuple(spot)].set(low).at[tuple(neighbour)].set(largest)


def levels(own_key, extent, cuts, low, largest):
    level = 1.0
    for dim, shards_of in cuts:
        steps = jax.random.uniform(jax.random.fold_in(jax.random.fold_in(own_key, 6), dim), (shards_of,), jnp.float32, low / len(cuts), largest / len(cuts))
        level = level * jnp.repeat(jnp.exp(steps), extent[dim] // shards_of).reshape((-1,) + (1,) * (len(extent) - 1 - dim))
    return level


def cumulative_ranks(count, skew):
    portions = [(1 << 20) // math.isqrt(standing ** skew) + 1 for standing in range(1, count + 1)]
    scale = 1 + sum(portions) // (1 << 30)
    return np.cumsum(np.array([max(1, weight // scale) for weight in portions]))


def skewed_ids(key, extent, count, skew):
    grid = cumulative_ranks(count, skew)
    pick = jax.random.randint(jax.random.fold_in(key, 1), extent, 0, int(grid[count - 1]))
    grade = jnp.searchsorted(jnp.asarray(grid, jnp.int32), pick, side="right")
    return jax.random.permutation(jax.random.fold_in(key, 2), count)[grade].astype(jnp.int32)


def noise(rng, shape, scale, reach, pieces=(), kind=jnp.bfloat16):
    values = jax.random.normal(rng, shape, jnp.float32) * scale
    if len(pieces) > 0:
        values = levels(rng, shape, pieces, -0.22, 0.18) * values
    return jnp.clip(values, min=-reach, max=reach).astype(kind)


def setup_inputs(seed: int = 0) -> dict:
    seeds = jax.random.split(jax.random.key(seed), 16)
    actor_rows = noise(seeds[0], (TOKEN_ROWS, MODEL_WIDTH), 1.0, 6.0, ((0, 16), (1, 8)))
    route_counts = draw_route_counts(jax.random.fold_in(seeds[15], 71), 0)
    targets = with_ends(skewed_ids(seeds[2], (TOKEN_ROWS,), VOCAB, 2), jax.random.fold_in(seeds[2], 3), 0, VOCAB - 1).astype(jnp.int32)
    pair_index = draw_pair_index(jax.random.fold_in(seeds[15], 71), 0)
    attn_gain = jnp.clip(1.0 + 0.15 * jax.random.normal(seeds[4], (MODEL_WIDTH,), jnp.float32), 0.25, 1.75)
    w_query = noise(seeds[5], (MODEL_WIDTH, QUERY_HEADS * HEAD_SIZE), MODEL_WIDTH ** -0.5, 0.0546875, ((0, 8), (1, 16)))
    key_weight = noise(seeds[6], (MODEL_WIDTH, KEY_VALUE_HEADS * HEAD_SIZE), MODEL_WIDTH ** -0.5, 0.0546875, ((0, 8),))
    value_weight = noise(seeds[7], (MODEL_WIDTH, KEY_VALUE_HEADS * HEAD_SIZE), MODEL_WIDTH ** -0.5, 0.0546875, ((0, 8),))
    w_out = noise(seeds[8], (QUERY_HEADS * HEAD_SIZE, MODEL_WIDTH), (QUERY_HEADS * HEAD_SIZE) ** -0.5, 0.0546875, ((0, 16), (1, 8)))
    mlp_gain = jnp.clip(1.0 + 0.15 * jax.random.normal(seeds[9], (MODEL_WIDTH,), jnp.float32), 0.25, 1.75)
    w_gate = noise(seeds[10], (MODEL_WIDTH, FF), MODEL_WIDTH ** -0.5, 0.0546875, ((0, 8), (1, 16)))
    w_up = noise(seeds[11], (MODEL_WIDTH, FF), MODEL_WIDTH ** -0.5, 0.0546875, ((0, 8), (1, 16)))
    w_down = noise(seeds[12], (FF, MODEL_WIDTH), FF ** -0.5, 0.046875, ((0, 16), (1, 8)))
    final_gain = jnp.clip(1.0 + 0.15 * jax.random.normal(seeds[13], (MODEL_WIDTH,), jnp.float32), 0.25, 1.75)
    w_vocab = noise(seeds[14], (MODEL_WIDTH, VOCAB), (MODEL_WIDTH // 9) ** -0.5, 0.15625, ((0, 8), (1, 16)))
    return {"actor_rows": actor_rows, "route_counts": route_counts, "targets": targets, "pair_index": pair_index, "attn_gain": attn_gain, "w_query": w_query, "key_weight": key_weight, "value_weight": value_weight, "w_out": w_out, "mlp_gain": mlp_gain, "w_gate": w_gate, "w_up": w_up, "w_down": w_down, "final_gain": final_gain, "w_vocab": w_vocab}


def route_tables(route_counts, row_count):
    group_count = route_counts.shape[0]
    all_rows = row_count * group_count
    actor_start = (jnp.cumsum(route_counts, axis=1) - route_counts).astype(jnp.int32)
    ref_start = (jnp.cumsum(route_counts, axis=0) - route_counts).astype(jnp.int32)
    row_index = jnp.arange(all_rows, dtype=jnp.int32)
    group_of = (row_index // row_count).astype(jnp.int32)
    local_pos = (row_index % row_count).astype(jnp.int32)
    piece_start = ref_start.T[group_of]
    piece_length = route_counts.T[group_of]
    piece_anchor = actor_start.T[group_of]
    inside = ((local_pos[:, None] >= piece_start) & (local_pos[:, None] < piece_start + piece_length)).astype(jnp.int32)
    actor_ids = jnp.arange(group_count, dtype=jnp.int32)[None, :]
    sequence_position = lax.optimization_barrier(jnp.sum(inside * (local_pos[:, None] - piece_start), axis=1)).astype(jnp.int32)
    source = (lax.optimization_barrier(jnp.sum(inside * (actor_ids * row_count + piece_anchor), axis=1)).astype(jnp.int32) + sequence_position).astype(jnp.int32)
    seq_id = lax.optimization_barrier(jnp.sum(inside * (actor_ids * group_count + group_of[:, None]), axis=1)).astype(jnp.int32)
    source_actor = lax.optimization_barrier(jnp.sum(inside * actor_ids, axis=1)).astype(jnp.int32)
    return (source, source_actor, seq_id, sequence_position, ref_start, actor_start)

def apply_rotary(vectors, positions):
    head_dim = vectors.shape[-1]
    half_dim = head_dim // 2
    exponent = jnp.arange(half_dim, dtype=jnp.float32) * (-2.0 / head_dim)
    frequency = jnp.power(jnp.float32(1000000.0), exponent)
    angle = positions.astype(jnp.float32)[:, None] * frequency[None, :]
    cosine = jnp.cos(angle)[:, None, :]
    sine_part = jnp.sin(angle)[:, None, :]
    first_half = vectors[..., :half_dim]
    second_half = vectors[..., half_dim:]
    return jnp.concatenate([first_half * cosine - second_half * sine_part, second_half * cosine + first_half * sine_part], axis=-1)

def rms_rows(values, gain_part):
    inverse_rms = lax.rsqrt(lax.optimization_barrier(jnp.mean(values * values, axis=1)) + 1e-05)
    return (values * inverse_rms[:, None] * gain_part[None, :]).astype(jnp.bfloat16)

def block_sum(inputs, matrix, block_count):
    block_width = inputs.shape[1] // block_count
    running = jnp.zeros((inputs.shape[0], matrix.shape[1]), jnp.float32)
    for block_id in range(block_count):
        product = jnp.dot(inputs[:, block_id * block_width:(block_id + 1) * block_width], matrix[block_id * block_width:(block_id + 1) * block_width], preferred_element_type=jnp.float32)
        running = running + lax.optimization_barrier(product.astype(jnp.bfloat16)).astype(jnp.float32)
    return running

def pair_table(token_logp, pair_index, route_counts, ref_start, row_count, cap_size):
    group_count = route_counts.shape[0]
    actor_of = (pair_index // group_count).astype(jnp.int32)
    block_of = (pair_index % group_count).astype(jnp.int32)
    length = route_counts[actor_of, block_of]
    begin_row = block_of * row_count + ref_start[actor_of, block_of]
    offsets = jnp.arange(cap_size, dtype=jnp.int32)
    where_at = jnp.clip(begin_row[..., None] + offsets, 0, token_logp.shape[0] - 1).astype(jnp.int32)
    picked = jnp.take(token_logp, where_at)
    masked = jnp.where(offsets < length[..., None], picked, jnp.zeros_like(picked))
    return masked.reshape(pair_index.shape[0], 2 * cap_size)

def reference(actor_rows, route_counts, targets, pair_index, attn_gain, w_query, key_weight, value_weight, w_out, mlp_gain, w_gate, w_up, w_down, final_gain, w_vocab):
    source, source_actor, seq_id, sequence_position, ref_start, actor_start = route_tables(route_counts, ROWS)
    ref_rows = jnp.take(actor_rows, source, axis=0)
    attn_in = rms_rows(ref_rows.astype(jnp.float32), attn_gain)
    query = block_sum(attn_in, w_query, N_TP)
    key_rows_full = block_sum(attn_in, key_weight, N_TP)
    value_rows_full = block_sum(attn_in, value_weight, N_TP)
    query_rot = apply_rotary(query.reshape(TOKEN_ROWS, QUERY_HEADS, HEAD_SIZE), sequence_position).astype(jnp.bfloat16)
    rotated_key = apply_rotary(key_rows_full.reshape(TOKEN_ROWS, KEY_VALUE_HEADS, HEAD_SIZE), sequence_position).astype(jnp.bfloat16)
    value_bfloat = value_rows_full.reshape(TOKEN_ROWS, KEY_VALUE_HEADS, HEAD_SIZE).astype(jnp.bfloat16)
    heads_per_group = QUERY_HEADS // KEY_VALUE_HEADS
    key_wide = jnp.repeat(rotated_key, heads_per_group, axis=1).astype(jnp.float32).reshape(GROUPS, ROWS, QUERY_HEADS, HEAD_SIZE)
    value_wide = jnp.repeat(value_bfloat, heads_per_group, axis=1).astype(jnp.float32).reshape(GROUPS, ROWS, QUERY_HEADS, HEAD_SIZE)
    query_blocks = query_rot.astype(jnp.float32).reshape(GROUPS, ROWS, QUERY_HEADS, HEAD_SIZE)
    scores = jnp.einsum('grhd,gshd->ghrs', query_blocks, key_wide) / math.sqrt(HEAD_SIZE)
    seq_blocks = seq_id.reshape(GROUPS, ROWS)
    row_ids = jnp.arange(ROWS, dtype=jnp.int32)
    allowed = (seq_blocks[:, :, None] == seq_blocks[:, None, :]) & (row_ids[:, None] >= row_ids[None, :])[None]
    weights = jnp.exp(scores) * allowed[:, None].astype(jnp.float32)
    probs = (weights / lax.optimization_barrier(jnp.sum(weights, axis=-1, keepdims=True))).astype(jnp.bfloat16)
    context = jnp.einsum('ghrs,gshd->grhd', probs.astype(jnp.float32), value_wide).astype(jnp.bfloat16).reshape(TOKEN_ROWS, QUERY_HEADS * HEAD_SIZE)
    attn_out = block_sum(context, w_out, N_GRP)
    mid = (ref_rows.astype(jnp.float32) + attn_out).astype(jnp.bfloat16)
    mlp_in = rms_rows(mid.astype(jnp.float32), mlp_gain)
    gate = block_sum(mlp_in, w_gate, N_TP)
    up_sum = block_sum(mlp_in, w_up, N_TP)
    hidden = (jax.nn.silu(gate) * up_sum).astype(jnp.bfloat16)
    final_rows = (mid.astype(jnp.float32) + block_sum(hidden, w_down, N_GRP)).astype(jnp.bfloat16)
    normed = rms_rows(final_rows.astype(jnp.float32), final_gain)
    logits = block_sum(normed, w_vocab, N_TP)
    target_logit = jnp.take_along_axis(logits, targets[:, None], axis=1)[:, 0]
    token_logp = target_logit - jnp.log(lax.optimization_barrier(jnp.sum(jnp.exp(logits), axis=1)))
    pair_scores = pair_table(token_logp, pair_index, route_counts, ref_start, ROWS, CAP)
    return (final_rows, pair_scores)
```

```python
import functools
import math

import jax
import jax.numpy as jnp
from jax import lax
from jax.experimental import pallas as pl
from jax.experimental.pallas import tpu as pltpu
from jax.sharding import PartitionSpec as P

MODEL_WIDTH = 12288
QUERY_HEADS = 96
KEY_VALUE_HEADS = 8
HEAD_SIZE = 128
SIDE = 4
CORES = 2


def coords(device):
    grp, tp = divmod(device, SIDE * CORES)
    return grp // SIDE, grp % SIDE, tp // CORES, tp % CORES


def permute(value, place):
    pairs = []
    for device in range(SIDE * SIDE * SIDE * CORES):
        x, z, y, c = place(*coords(device))
        target = ((x % SIDE) * SIDE + z % SIDE) * SIDE * CORES + (y % SIDE) * CORES + c
        pairs.append((device, target))
    return lax.ppermute(value, ("grp", "tp"), pairs)


def send_first(value, step):
    return permute(
        value, lambda x, z, y, c: (x + step, z, y, c) if c == 0 else (x, z + step, y, c)
    )


def send_second(value, step):
    return permute(
        value, lambda x, z, y, c: (x, z + step, y, c) if c == 0 else (x + step, z, y, c)
    )


def send_y(value, step):
    return permute(value, lambda x, z, y, c: (x, z, y + step, c))


def swap_cores(value):
    return permute(value, lambda x, z, y, c: (x, z, y, 1 - c))


def call(kernel, outs, scratch, *operands, places=None, limit=24):
    places = places or [pltpu.VMEM] * len(operands)
    return pl.pallas_call(
        kernel,
        out_shape=[jax.ShapeDtypeStruct(shape, dtype) for shape, dtype in outs],
        in_specs=[pl.BlockSpec(memory_space=place) for place in places],
        out_specs=[pl.BlockSpec(memory_space=pltpu.VMEM) for _ in outs],
        scratch_shapes=scratch,
        compiler_params=pltpu.CompilerParams(vmem_limit_bytes=limit * 1024 * 1024),
    )(*operands)


def pack_squares(squares):
    lane = lax.broadcasted_iota(jnp.int32, (squares.shape[0], 128), 1)
    high = squares.astype(jnp.bfloat16).astype(jnp.float32)
    tile = jnp.where(lane == 0, high, jnp.where(lane == 1, squares - high, 0.0))
    return tile.astype(jnp.bfloat16)


def order_kernel(where, first, second, third, fourth, chunk):
    rows = first.shape[0]
    for step, part in enumerate((first, second, third, fourth)):
        at = pl.multiple_of(lax.rem(where[1] + step, SIDE) * rows, rows)
        chunk[pl.ds(at, rows), :] = part[...]


def project_kernel(
    widths, where, first, second, third, fourth, gain, *refs
):
    matrices, refs = refs[: len(widths)], refs[len(widths) :]
    mine, other, scaled, held, sem = refs
    half = mine.shape[1]
    rows = first.shape[0]
    tiles, start = [], 0
    for matrix, width in zip(matrices, widths):
        for at in range(0, width, 256):
            size = min(256, width - at)
            tiles.append((matrix, at, start + at, size))
        start += width
    copies = [
        pltpu.make_async_copy(
            matrix.at[:, pl.ds(at, size)], held.at[:, pl.ds(to, size)], sem.at[number]
        )
        for number, (matrix, at, to, size) in enumerate(tiles)
    ]
    for copy in copies:
        copy.start()
    p, y, c = where[0], where[2], where[3]
    slots = [lax.rem(p + step + SIDE - y, SIDE) for step in range(SIDE)]

    def store(step, to, size, values):
        lower, upper = values[:half], values[half:]
        mine[slots[step], :, to : to + size] = jnp.where(c == 0, lower, upper)
        other[slots[step], :, to : to + size] = jnp.where(c == 0, upper, lower)

    for step, chunk in enumerate((first, second, third, fourth)):
        wide = chunk[...].astype(jnp.float32)
        scaled[step * rows : (step + 1) * rows, :] = (wide * gain[...]).astype(jnp.bfloat16)
        store(step, start, 128, pack_squares(jnp.sum(wide * wide, axis=1, keepdims=True)))
    for copy, (_, _, to, size) in zip(copies, tiles):
        copy.wait()
        product = jnp.dot(
            scaled[...], held[:, to : to + size], preferred_element_type=jnp.float32
        ).astype(jnp.bfloat16)
        for step in range(SIDE):
            store(step, to, size, product[step * rows : (step + 1) * rows])


def pair_kernel(mine, other, own, *sent):
    width = mine.shape[2] - 128
    for step, out in enumerate((own,) + sent):
        left = mine[step].astype(jnp.float32)
        right = other[step].astype(jnp.float32)
        total = left + right
        out[:, :width] = total[:, :width].astype(out.dtype)
        squares = jnp.sum(total[:, width:], axis=1, keepdims=True)
        out[:, width:] = pack_squares(squares).astype(out.dtype)


def normed_sum(own, parts):
    width = own.shape[1] - 128
    total = own[...]
    for part in parts:
        total = total + part[...].astype(jnp.float32)
    squares = jnp.sum(total[:, width:], axis=1, keepdims=True)
    return total[:, :width] * lax.rsqrt(squares / MODEL_WIDTH + 1e-05)


def attention_kernel(own, first, second, third, cosine, sine, allowed, context):
    projected = normed_sum(own, (first, second, third))
    cosine, sine, allowed = cosine[...], sine[...], allowed[...]
    half = HEAD_SIZE // 2

    def rotate(vectors):
        turned = jnp.concatenate([vectors[:, half:], vectors[:, :half]], axis=1)
        return (vectors * cosine + turned * sine).astype(jnp.bfloat16)

    key_at = context.shape[1]
    key = rotate(projected[:, key_at : key_at + HEAD_SIZE])
    value = projected[:, key_at + HEAD_SIZE :].astype(jnp.bfloat16)
    for at in range(0, key_at, HEAD_SIZE):
        query = rotate(projected[:, at : at + HEAD_SIZE])
        scores = lax.dot_general(
            query, key, (((1,), (1,)), ((), ())), preferred_element_type=jnp.float32
        ) * (1.0 / math.sqrt(HEAD_SIZE))
        weights = jnp.where(allowed > 0.0, jnp.exp(scores), 0.0)
        probs = (weights / jnp.sum(weights, axis=1, keepdims=True)).astype(jnp.bfloat16)
        context[:, at : at + HEAD_SIZE] = jnp.dot(
            probs, value, preferred_element_type=jnp.float32
        ).astype(jnp.bfloat16)


def hidden_kernel(own, first, second, third, hidden):
    both = normed_sum(own, (first, second, third))
    width = hidden.shape[1]
    gate, up = both[:, :width], both[:, width:]
    hidden[...] = (gate / (1.0 + jnp.exp(-gate)) * up).astype(jnp.bfloat16)


def score_kernel(own, first, second, third, target, sums):
    logits = normed_sum(own, (first, second, third))
    rows = logits.shape[0]
    columns = lax.broadcasted_iota(jnp.int32, logits.shape, 1)
    totals = jnp.sum(jnp.exp(logits), axis=1, keepdims=True)
    chosen = jnp.sum(jnp.where(columns == target[...], logits, 0.0), axis=1, keepdims=True)
    line = lax.broadcasted_iota(jnp.int32, (rows, 128), 0)
    lane = lax.broadcasted_iota(jnp.int32, (rows, 128), 1)
    sums[...] = jnp.zeros_like(sums)
    sums[0:1, :] = jnp.sum(jnp.where(line == lane, totals, 0.0), axis=0, keepdims=True)
    sums[1:2, :] = jnp.sum(jnp.where(line == lane, chosen, 0.0), axis=0, keepdims=True)


def project_out_kernel(step, where, *refs):
    mine, theirs, matrix, out, rows, held, sem = refs[:4], refs[4:8], *refs[8:]
    size = min(512, matrix.shape[1])
    copies = [
        pltpu.make_async_copy(
            matrix.at[:, pl.ds(at, size)], held.at[:, pl.ds(at, size)], sem.at[at // size]
        )
        for at in range(0, matrix.shape[1], size)
    ]
    for copy in copies:
        copy.start()
    p, y, c = where[0], where[2], where[3]
    half = mine[0].shape[0]
    index = lax.rem(p + step + SIDE - y, SIDE)
    for number in range(SIDE):

        @pl.when(index == number)
        def _():
            left, right = mine[number][...], theirs[number][...]
            rows[:half, :] = jnp.where(c == 0, left, right)
            rows[half:, :] = jnp.where(c == 0, right, left)

    for copy, at in zip(copies, range(0, matrix.shape[1], size)):
        copy.wait()
        out[:, at : at + size] = jnp.dot(
            rows[...], held[:, at : at + size], preferred_element_type=jnp.float32
        ).astype(out.dtype)


def scatter_kernel(where, own, first, second, third, kept, *sent):
    rows = kept.shape[0]
    for step, out in enumerate((kept,) + sent):
        at = pl.multiple_of(lax.rem(where[1] + step, SIDE) * rows, rows)
        total = own[pl.ds(at, rows), :]
        for part in (first, second, third):
            total = total + part[pl.ds(at, rows), :].astype(jnp.float32)
        out[...] = total.astype(out.dtype)


def per_device(
    actor_rows,
    route_counts,
    targets,
    pair_index,
    attn_gain,
    w_query,
    key_weight,
    value_weight,
    w_out,
    mlp_gain,
    w_gate,
    w_up,
    w_down,
    final_gain,
    w_vocab,
):
    grp = lax.axis_index("grp")
    tp = lax.axis_index("tp")
    x, z, y, c = grp // SIDE, grp % SIDE, tp // CORES, tp % CORES
    p = jnp.where(c == 0, x, z)
    q = jnp.where(c == 0, z, x)
    group_count = route_counts.shape[0]
    row_count, feat_width = actor_rows.shape
    all_rows = row_count * group_count
    slice_rows = all_rows // (SIDE * CORES)
    cap_size = 2 * row_count // group_count

    where = jnp.stack([p, q, y, c]).astype(jnp.int32)
    bf16, f32 = jnp.bfloat16, jnp.float32
    in_smem = [pltpu.SMEM]
    in_vmem = [pltpu.VMEM]
    anywhere = [pl.ANY]
    sent_bf16 = [bf16] * (SIDE - 1)

    def gather_group(parts):
        (chunk,) = call(
            order_kernel,
            [((SIDE * row_count, feat_width), bf16)],
            [],
            where,
            *parts,
            places=in_smem + in_vmem * SIDE,
        )
        got = {step: send_first(chunk, -step) for step in (1, 3, 2)}
        return [chunk] + [got[step] for step in (1, 2, 3)]

    def gather_rows(block):
        got = {step: send_second(block, -step) for step in (1, 3, 2)}
        return gather_group([block] + [got[step] for step in (1, 2, 3)])

    def project(chunks, gain, matrices):
        widths = tuple(matrix.shape[1] for matrix in matrices)
        total = sum(widths) + 128
        tiles = sum(-(-width // 256) for width in widths)
        halves = (SIDE, slice_rows, total)
        mine, other = call(
            functools.partial(project_kernel, widths),
            [(halves, bf16), (halves, bf16)],
            [
                pltpu.VMEM((all_rows, feat_width), bf16),
                pltpu.VMEM((feat_width, total - 128), bf16),
                pltpu.SemaphoreType.DMA((tiles,)),
            ],
            where,
            *chunks,
            gain[None, :],
            *matrices,
            places=in_smem + in_vmem * (SIDE + 1) + anywhere * len(matrices),
        )
        own, *sent = call(
            pair_kernel,
            [((slice_rows, total), kind) for kind in [f32] + sent_bf16],
            [],
            mine,
            swap_cores(other),
        )
        return [own] + [send_y(sent[step - 1], step) for step in (1, 3, 2)]

    def gather_slices(block):
        got = {0: block} | {step: send_y(block, -step) for step in (1, 3, 2)}
        mine = [got[step] for step in range(SIDE)]
        return mine + [swap_cores(part) for part in mine]

    def project_out(blocks, matrix):
        wide = matrix.shape[1]
        parts = []
        for step in (2, 1, 3, 0):
            (part,) = call(
                functools.partial(project_out_kernel, step),
                [((SIDE * row_count, wide), bf16 if step else f32)],
                [
                    pltpu.VMEM((SIDE * row_count, matrix.shape[0]), bf16),
                    pltpu.VMEM(matrix.shape, bf16),
                    pltpu.SemaphoreType.DMA((max(wide // 512, 1),)),
                ],
                where,
                *blocks,
                matrix,
                places=in_smem + in_vmem * len(blocks) + anywhere,
            )
            parts.append(send_first(part, step) if step else part)
        kept, *sent = call(
            scatter_kernel,
            [((row_count, wide), kind) for kind in [f32] + sent_bf16],
            [],
            where,
            parts[-1],
            *parts[:-1],
            places=in_smem + in_vmem * SIDE,
        )
        for step in (1, 3, 2):
            kept = kept + send_second(sent[step - 1], step).astype(f32)
        return kept

    counts = route_counts
    actor_start = jnp.cumsum(counts, axis=1) - counts
    ref_start = jnp.cumsum(counts, axis=0) - counts
    blocks = jnp.arange(group_count, dtype=jnp.int32)
    local = jnp.arange(row_count, dtype=jnp.int32)

    def slice_tables():
        first = tp * (slice_rows // row_count)
        starts = lax.dynamic_slice_in_dim(actor_start, first, slice_rows // row_count, 0)
        lengths = lax.dynamic_slice_in_dim(counts, first, slice_rows // row_count, 0)
        ref = lax.dynamic_slice_in_dim(ref_start, first, slice_rows // row_count, 0)
        offset = local[None, :, None] - starts[:, None, :]
        inside = ((offset >= 0) & (offset < lengths[:, None, :])).astype(jnp.int32)
        position = jnp.sum(inside * offset, axis=2).reshape(-1)
        piece = jnp.sum(inside * blocks, axis=2)
        ref_row = jnp.sum(
            inside * (blocks * row_count + ref[:, None, :] + offset), axis=2
        ).reshape(-1)
        sequence = (piece + group_count * jnp.arange(slice_rows // row_count)[:, None]).reshape(-1)
        return position, sequence, ref_row

    position, sequence, ref_row = slice_tables()
    all_ids = jnp.arange(all_rows, dtype=jnp.int32)
    slice_targets = jnp.sum(
        jnp.where(ref_row[:, None] == all_ids[None, :], targets[None, :], 0), axis=1
    )

    first_parts = [
        permute(
            actor_rows,
            lambda x, z, y, c, s=step: (x, z - s, y, c) if c == 0 else (z - s, x, y, c),
        )
        if step
        else permute(
            actor_rows, lambda x, z, y, c: (x, z, y, c) if c == 0 else (z, x, y, c)
        )
        for step in range(SIDE)
    ]
    block_rows = first_parts[0]
    attn_chunks = gather_group(first_parts)

    local_heads = w_query.shape[1] // HEAD_SIZE
    key_value_head = grp * local_heads // (QUERY_HEADS // KEY_VALUE_HEADS)
    key_cols = lax.dynamic_slice_in_dim(key_weight, key_value_head * HEAD_SIZE, HEAD_SIZE, 1)
    value_cols = lax.dynamic_slice_in_dim(value_weight, key_value_head * HEAD_SIZE, HEAD_SIZE, 1)
    projected = project(attn_chunks, attn_gain, (w_query, key_cols, value_cols))
    exponent = jnp.arange(HEAD_SIZE // 2, dtype=jnp.float32) * (-2.0 / HEAD_SIZE)
    frequency = jnp.power(jnp.float32(1000000.0), exponent)
    angle = position.astype(jnp.float32)[:, None] * frequency[None, :]
    cosine, sine = jnp.cos(angle), jnp.sin(angle)
    ids = jnp.arange(slice_rows, dtype=jnp.int32)
    allowed = (
        (sequence[:, None] == sequence[None, :]) & (ids[:, None] >= ids[None, :])
    ).astype(jnp.float32)
    (context,) = call(
        attention_kernel,
        [((slice_rows, local_heads * HEAD_SIZE), bf16)],
        [],
        *projected,
        jnp.concatenate([cosine, cosine], axis=1),
        jnp.concatenate([-sine, sine], axis=1),
        allowed,
    )
    attn_out = project_out(gather_slices(context), w_out)
    mid = (block_rows.astype(jnp.float32) + attn_out).astype(jnp.bfloat16)

    (hidden,) = call(
        hidden_kernel,
        [((slice_rows, w_gate.shape[1]), bf16)],
        [],
        *project(gather_rows(mid), mlp_gain, (w_gate, w_up)),
    )
    mlp_out = project_out(gather_slices(hidden), w_down)
    final_block = (mid.astype(jnp.float32) + mlp_out).astype(jnp.bfloat16)
    final_chunks = gather_rows(final_block)
    (sums,) = call(
        score_kernel,
        [((8, 128), f32)],
        [],
        *project(final_chunks, final_gain, (w_vocab,)),
        (slice_targets - grp * w_vocab.shape[1])[:, None],
    )

    my_starts = lax.dynamic_index_in_dim(ref_start, grp, 1, keepdims=False)
    my_lengths = lax.dynamic_index_in_dim(counts, grp, 1, keepdims=False)
    my_actor = lax.dynamic_index_in_dim(actor_start, grp, 1, keepdims=False)
    offset = local[:, None] - my_starts[None, :]
    inside = ((offset >= 0) & (offset < my_lengths[None, :])).astype(jnp.int32)
    source = jnp.sum(inside * (blocks * row_count + my_actor + offset), axis=1)
    final_rows = None
    for step, chunk in enumerate(final_chunks):
        rows = ((p + step) % SIDE) * chunk.shape[0] + jnp.arange(chunk.shape[0])
        chosen = (source[:, None] == rows[None, :]).astype(jnp.bfloat16)
        part = jnp.dot(chosen, chunk, preferred_element_type=jnp.float32)
        final_rows = part if final_rows is None else final_rows + part
    final_rows = final_rows.astype(jnp.bfloat16)

    for send in (send_first, send_second):
        parts = [send(sums, step) for step in (1, 3, 2)]
        sums = sums + parts[0] + parts[1] + parts[2]
    slice_logp = sums[1:2, :slice_rows] - jnp.log(sums[0:1, :slice_rows])
    other = swap_cores(slice_logp)
    chip = jnp.concatenate(
        [jnp.where(c == 0, slice_logp, other), jnp.where(c == 0, other, slice_logp)], axis=1
    )
    got = [chip] + [send_y(chip, -step) for step in (1, 2, 3)]
    token_logp = jnp.concatenate(got, axis=1).reshape(-1)

    actor_of = pair_index[0] // group_count
    block_of = pair_index[0] % group_count
    hit = (actor_of[:, None, None] == blocks[None, :, None]) & (
        block_of[:, None, None] == blocks[None, None, :]
    )
    length = jnp.sum(jnp.where(hit, counts[None], 0), axis=(1, 2))
    begin = actor_of * row_count + jnp.sum(jnp.where(hit, actor_start[None], 0), axis=(1, 2))
    offsets = jnp.arange(cap_size, dtype=jnp.int32)
    wanted = jnp.where(offsets[None, :] < length[:, None], begin[:, None] + offsets[None, :], -1)
    actual = (all_ids + y * (CORES * slice_rows)) % all_rows
    scores = jnp.sum(
        jnp.where(wanted.reshape(-1, 1) == actual[None, :], token_logp[None, :], 0.0), axis=1
    )
    return final_rows, scores.reshape(1, 2 * cap_size)


def solution(mesh):
    in_specs = (
        P("grp", "tp"),
        P(),
        P(),
        P(("grp", "tp"), None),
        P("tp"),
        P("tp", "grp"),
        P("tp", None),
        P("tp", None),
        P("grp", "tp"),
        P("tp"),
        P("tp", "grp"),
        P("tp", "grp"),
        P("grp", "tp"),
        P("tp"),
        P("tp", "grp"),
    )
    out_specs = (P("grp", "tp"), P(("grp", "tp"), None))
    return jax.shard_map(
        per_device, mesh=mesh, in_specs=in_specs, out_specs=out_specs, check_vma=False
    )
```

```python
import functools
import math

import jax
import jax.numpy as jnp
from jax import lax
from jax.experimental import pallas as pl
from jax.experimental.pallas import tpu as pltpu
from jax.sharding import PartitionSpec as P

MODEL_WIDTH = 12288
QUERY_HEADS = 96
KEY_VALUE_HEADS = 8
HEAD_SIZE = 128
SIDE = 4
CORES = 2


def coords(device):
    grp, tp = divmod(device, SIDE * CORES)
    return grp // SIDE, grp % SIDE, tp // CORES, tp % CORES


def permute(value, place):
    pairs = []
    for device in range(SIDE * SIDE * SIDE * CORES):
        x, z, y, c = place(*coords(device))
        target = ((x % SIDE) * SIDE + z % SIDE) * SIDE * CORES + (y % SIDE) * CORES + c
        pairs.append((device, target))
    return lax.ppermute(value, ("grp", "tp"), pairs)


def send_first(value, step):
    return permute(
        value, lambda x, z, y, c: (x + step, z, y, c) if c == 0 else (x, z + step, y, c)
    )


def send_second(value, step):
    return permute(
        value, lambda x, z, y, c: (x, z + step, y, c) if c == 0 else (x + step, z, y, c)
    )


def exchange_second(value, partner):
    return permute(
        value, lambda x, z, y, c: (x, partner(z), y, c) if c == 0 else (partner(x), z, y, c)
    )


def send_y(value, step):
    return permute(value, lambda x, z, y, c: (x, z, y + step, c))


def swap_cores(value):
    return permute(value, lambda x, z, y, c: (x, z, y, 1 - c))


def call(kernel, outs, scratch, *operands, places=None, after=None, limit=24):
    places = places or [pltpu.VMEM] * len(operands)
    body, count = kernel, len(operands)
    if after is not None:
        operands, places = operands + (after,), places + [pl.ANY]

        def body(*refs):
            kernel(*refs[:count], *refs[count + 1 :])

    return pl.pallas_call(
        body,
        out_shape=[jax.ShapeDtypeStruct(shape, dtype) for shape, dtype in outs],
        in_specs=[pl.BlockSpec(memory_space=place) for place in places],
        out_specs=[pl.BlockSpec(memory_space=pltpu.VMEM) for _ in outs],
        scratch_shapes=scratch,
        compiler_params=pltpu.CompilerParams(vmem_limit_bytes=limit * 1024 * 1024),
    )(*operands)


def pack_squares(squares):
    lane = lax.broadcasted_iota(jnp.int32, (squares.shape[0], 128), 1)
    high = squares.astype(jnp.bfloat16).astype(jnp.float32)
    tile = jnp.where(lane == 0, high, jnp.where(lane == 1, squares - high, 0.0))
    return tile.astype(jnp.bfloat16)


def order_kernel(where, first, second, third, fourth, chunk):
    rows = first.shape[0]
    for step, part in enumerate((first, second, third, fourth)):
        at = pl.multiple_of(lax.rem(where[1] + step, SIDE) * rows, rows)
        chunk[pl.ds(at, rows), :] = part[...]


def block_place(where, step, number):
    p, y, c = where[0], where[2], where[3]
    chunk = lax.rem(p + step, SIDE)
    x = jnp.where(c == 0, chunk, number)
    z = jnp.where(c == 0, number, chunk)
    return lax.rem(x + SIDE - y, SIDE), z // CORES, lax.rem(z, CORES)


def products(chunk, gain, matrices, out):
    wide = chunk[...].astype(jnp.float32)
    scaled = (wide * gain[...]).astype(jnp.bfloat16)
    start = 0
    for matrix in matrices:
        width = matrix.shape[1]
        for at in range(0, width, 256):
            size = min(256, width - at)
            out[:, start + at : start + at + size] = jnp.dot(
                scaled, matrix[:, at : at + size], preferred_element_type=jnp.float32
            ).astype(out.dtype)
        start += width
    out[:, start:] = pack_squares(jnp.sum(wide * wide, axis=1, keepdims=True))


def project_kernel(chunk, gain, *refs):
    products(chunk, gain, refs[:-1], refs[-1])


def project_last_kernel(order, where, *refs):
    earlier, chunk, gain, matrices = refs[:3], refs[3], refs[4], refs[5:-3]
    mine, other, last = refs[-3:]
    products(chunk, gain, matrices, last)
    rows = mine.shape[1] // CORES
    c = where[3]
    for step, part in zip(order, earlier + (last,)):
        for number in range(SIDE):
            slot, half, place = block_place(where, step, number)
            at = pl.multiple_of(place * rows, rows)
            block = part[number * rows : (number + 1) * rows, :]

            @pl.when(half == c)
            def _():
                mine[slot, pl.ds(at, rows), :] = block

            @pl.when(half != c)
            def _():
                other[slot, pl.ds(at, rows), :] = block


def pair_kernel(mine, other, own, *sent):
    width = mine.shape[2] - 128
    for step, out in enumerate((own,) + sent):
        left = mine[step].astype(jnp.float32)
        right = other[step].astype(jnp.float32)
        total = left + right
        out[:, :width] = total[:, :width].astype(out.dtype)
        squares = jnp.sum(total[:, width:], axis=1, keepdims=True)
        out[:, width:] = pack_squares(squares).astype(out.dtype)


def normed_sum(own, parts):
    width = own.shape[1] - 128
    total = own[...]
    for part in parts:
        total = total + part[...].astype(jnp.float32)
    squares = jnp.sum(total[:, width:], axis=1, keepdims=True)
    return total[:, :width] * lax.rsqrt(squares / MODEL_WIDTH + 1e-05)


def attention_kernel(own, first, second, third, cosine, sine, allowed, context):
    projected = normed_sum(own, (first, second, third))
    cosine, sine, allowed = cosine[...], sine[...], allowed[...]
    half = HEAD_SIZE // 2

    def rotate(vectors):
        turned = jnp.concatenate([vectors[:, half:], vectors[:, :half]], axis=1)
        return (vectors * cosine + turned * sine).astype(jnp.bfloat16)

    key_at = context.shape[1]
    key = rotate(projected[:, key_at : key_at + HEAD_SIZE])
    value = projected[:, key_at + HEAD_SIZE :].astype(jnp.bfloat16)
    for at in range(0, key_at, HEAD_SIZE):
        query = rotate(projected[:, at : at + HEAD_SIZE])
        scores = lax.dot_general(
            query, key, (((1,), (1,)), ((), ())), preferred_element_type=jnp.float32
        ) * (1.0 / math.sqrt(HEAD_SIZE))
        weights = jnp.where(allowed > 0.0, jnp.exp(scores), 0.0)
        probs = (weights / jnp.sum(weights, axis=1, keepdims=True)).astype(jnp.bfloat16)
        context[:, at : at + HEAD_SIZE] = jnp.dot(
            probs, value, preferred_element_type=jnp.float32
        ).astype(jnp.bfloat16)


def hidden_kernel(own, first, second, third, hidden):
    both = normed_sum(own, (first, second, third))
    width = hidden.shape[1]
    gate, up = both[:, :width], both[:, width:]
    hidden[...] = (gate / (1.0 + jnp.exp(-gate)) * up).astype(jnp.bfloat16)


def score_kernel(own, first, second, third, target, sums):
    logits = normed_sum(own, (first, second, third))
    rows = logits.shape[0]
    columns = lax.broadcasted_iota(jnp.int32, logits.shape, 1)
    totals = jnp.sum(jnp.exp(logits), axis=1, keepdims=True)
    chosen = jnp.sum(jnp.where(columns == target[...], logits, 0.0), axis=1, keepdims=True)
    line = lax.broadcasted_iota(jnp.int32, (rows, 128), 0)
    lane = lax.broadcasted_iota(jnp.int32, (rows, 128), 1)
    sums[...] = jnp.zeros_like(sums)
    sums[0:1, :] = jnp.sum(jnp.where(line == lane, totals, 0.0), axis=0, keepdims=True)
    sums[1:2, :] = jnp.sum(jnp.where(line == lane, chosen, 0.0), axis=0, keepdims=True)


def project_out_kernel(order, where, *refs):
    mine, theirs, matrix, outs, rows = refs[:4], refs[4:8], refs[8], refs[9:-1], refs[-1]
    c = where[3]
    size = mine[0].shape[0] // CORES
    lines = outs[0].shape[0]
    for position, step in enumerate(order):
        for number in range(SIDE):
            slot, half, place = block_place(where, step, number)
            at = pl.multiple_of(place * size, size)
            to = pl.ds(position * lines + number * size, size)
            for chip in range(SIDE):

                @pl.when((slot == chip) & (half == c))
                def _():
                    rows[to, :] = mine[chip][pl.ds(at, size), :]

                @pl.when((slot == chip) & (half != c))
                def _():
                    rows[to, :] = theirs[chip][pl.ds(at, size), :]

    tile = min(256, matrix.shape[1])
    for at in range(0, matrix.shape[1], tile):
        product = jnp.dot(
            rows[...], matrix[:, at : at + tile], preferred_element_type=jnp.float32
        )
        for position, out in enumerate(outs):
            out[:, at : at + tile] = product[position * lines : (position + 1) * lines].astype(
                out.dtype
            )


def sum_kernel(own, first, second, third, *halves):
    width = halves[0].shape[1]
    for number, out in enumerate(halves):
        at = slice(number * width, (number + 1) * width)
        total = own[:, at]
        for part in (first, second, third):
            total = total + part[:, at].astype(jnp.float32)
        out[...] = total.astype(out.dtype)


def add_kernel(left, left_got, right, right_got, left_out, right_out):
    for own, got, out in ((left, left_got, left_out), (right, right_got, right_out)):
        out[...] = (own[...].astype(jnp.float32) + got[...].astype(jnp.float32)).astype(out.dtype)


def residual_kernel(rows, left, left_got, right, right_got, out):
    width = left.shape[1]
    for number, (own, got) in enumerate(((left, left_got), (right, right_got))):
        at = slice(number * width, (number + 1) * width)
        change = own[...].astype(jnp.float32) + got[...].astype(jnp.float32)
        out[:, at] = (rows[:, at].astype(jnp.float32) + change).astype(out.dtype)


def per_device(
    actor_rows,
    route_counts,
    targets,
    pair_index,
    attn_gain,
    w_query,
    key_weight,
    value_weight,
    w_out,
    mlp_gain,
    w_gate,
    w_up,
    w_down,
    final_gain,
    w_vocab,
):
    grp = lax.axis_index("grp")
    tp = lax.axis_index("tp")
    x, z, y, c = grp // SIDE, grp % SIDE, tp // CORES, tp % CORES
    p = jnp.where(c == 0, x, z)
    q = jnp.where(c == 0, z, x)
    group_count = route_counts.shape[0]
    row_count, feat_width = actor_rows.shape
    all_rows = row_count * group_count
    slice_rows = all_rows // (SIDE * CORES)
    cap_size = 2 * row_count // group_count

    where = jnp.stack([p, q, y, c]).astype(jnp.int32)
    bf16, f32 = jnp.bfloat16, jnp.float32
    in_smem = [pltpu.SMEM]
    in_vmem = [pltpu.VMEM]
    sent_bf16 = [bf16] * (SIDE - 1)

    def line_chunk(block):
        got = {step: send_second(block, -step) for step in (1, 3, 2)}
        (chunk,) = call(
            order_kernel,
            [((SIDE * row_count, feat_width), bf16)],
            [],
            where,
            block,
            *(got[step] for step in (1, 2, 3)),
            places=in_smem + in_vmem * SIDE,
        )
        return chunk

    ORDER = (0, 1, 3, 2)

    def gather_chunks(chunk):
        return [chunk] + [send_first(chunk, -step) for step in ORDER[1:]]

    def project(chunks, gain, matrices):
        total = sum(matrix.shape[1] for matrix in matrices) + 128
        parts = []
        for chunk in chunks[:-1]:
            (part,) = call(
                project_kernel,
                [((chunk.shape[0], total), bf16)],
                [],
                chunk,
                gain,
                *matrices,
                after=parts[-1] if parts else None,
            )
            parts.append(part)
        halves = (SIDE, slice_rows, total)
        mine, other = call(
            functools.partial(project_last_kernel, ORDER),
            [(halves, bf16), (halves, bf16)],
            [pltpu.VMEM((chunks[-1].shape[0], total), bf16)],
            where,
            *parts,
            chunks[-1],
            gain,
            *matrices,
            places=in_smem + in_vmem * (SIDE + 1 + len(matrices)),
        )
        own, *sent = call(
            pair_kernel,
            [((slice_rows, total), kind) for kind in [f32] + sent_bf16],
            [],
            mine,
            swap_cores(other),
        )
        return [own] + [send_y(sent[step - 1], step) for step in ORDER[1:]]

    def gather_slices(block):
        got = {0: block} | {step: send_y(block, -step) for step in ORDER[1:]}
        mine = [got[step] for step in range(SIDE)]
        return mine + [swap_cores(part) for part in mine]

    def project_out(blocks, matrix, rows):
        wide = matrix.shape[1]
        order = (2, 1, 3, 0)
        lines = SIDE * row_count
        parts = call(
            functools.partial(project_out_kernel, order),
            [((lines, wide), bf16 if step else f32) for step in order],
            [pltpu.VMEM((all_rows, matrix.shape[0]), bf16)],
            where,
            *blocks,
            matrix,
            places=in_smem + in_vmem * (len(blocks) + 1),
        )
        parts = [send_first(part, step) if step else part for part, step in zip(parts, order)]
        half = ((SIDE * row_count, wide // 2), bf16)
        left, right = call(sum_kernel, [half, half], [], parts[-1], *parts[:-1])
        near, far = (lambda i: i ^ 1), (lambda i: SIDE - 1 - i)
        left, right = call(
            add_kernel,
            [half, half],
            [],
            left,
            exchange_second(left, near),
            right,
            exchange_second(right, far),
        )
        (result,) = call(
            residual_kernel,
            [(rows.shape, bf16)],
            [],
            rows,
            left,
            exchange_second(left, far),
            right,
            exchange_second(right, near),
        )
        return result

    counts = route_counts
    actor_start = jnp.cumsum(counts, axis=1) - counts
    ref_start = jnp.cumsum(counts, axis=0) - counts
    blocks = jnp.arange(group_count, dtype=jnp.int32)
    local = jnp.arange(row_count, dtype=jnp.int32)

    def slice_tables():
        first = tp * (slice_rows // row_count)
        starts = lax.dynamic_slice_in_dim(actor_start, first, slice_rows // row_count, 0)
        lengths = lax.dynamic_slice_in_dim(counts, first, slice_rows // row_count, 0)
        ref = lax.dynamic_slice_in_dim(ref_start, first, slice_rows // row_count, 0)
        offset = local[None, :, None] - starts[:, None, :]
        inside = ((offset >= 0) & (offset < lengths[:, None, :])).astype(jnp.int32)
        position = jnp.sum(inside * offset, axis=2).reshape(-1)
        piece = jnp.sum(inside * blocks, axis=2)
        ref_row = jnp.sum(
            inside * (blocks * row_count + ref[:, None, :] + offset), axis=2
        ).reshape(-1)
        sequence = (piece + group_count * jnp.arange(slice_rows // row_count)[:, None]).reshape(-1)
        return position, sequence, ref_row

    position, sequence, ref_row = slice_tables()
    all_ids = jnp.arange(all_rows, dtype=jnp.int32)
    exponent = jnp.arange(HEAD_SIZE // 2, dtype=jnp.float32) * (-2.0 / HEAD_SIZE)
    frequency = jnp.power(jnp.float32(1000000.0), exponent)
    angle = position.astype(jnp.float32)[:, None] * frequency[None, :]
    cosine, sine = jnp.cos(angle), jnp.sin(angle)
    ids = jnp.arange(slice_rows, dtype=jnp.int32)
    allowed = (
        (sequence[:, None] == sequence[None, :]) & (ids[:, None] >= ids[None, :])
    ).astype(jnp.float32)
    cosine = jnp.concatenate([cosine, cosine], axis=1)
    sine = jnp.concatenate([-sine, sine], axis=1)
    line_rows = line_chunk(actor_rows)

    local_heads = w_query.shape[1] // HEAD_SIZE
    key_value_head = grp * local_heads // (QUERY_HEADS // KEY_VALUE_HEADS)
    key_cols = lax.dynamic_slice_in_dim(key_weight, key_value_head * HEAD_SIZE, HEAD_SIZE, 1)
    value_cols = lax.dynamic_slice_in_dim(value_weight, key_value_head * HEAD_SIZE, HEAD_SIZE, 1)
    line_rows, counts, actor_start, ref_start, ref_row, pair_index = lax.optimization_barrier(
        (line_rows, counts, actor_start, ref_start, ref_row, pair_index)
    )
    attn_chunks = gather_chunks(line_rows)
    slice_targets = jnp.sum(
        jnp.where(ref_row[:, None] == all_ids[None, :], targets[None, :], 0), axis=1
    )
    my_starts = lax.dynamic_index_in_dim(ref_start, grp, 1, keepdims=False)
    my_lengths = lax.dynamic_index_in_dim(counts, grp, 1, keepdims=False)
    my_actor = lax.dynamic_index_in_dim(actor_start, grp, 1, keepdims=False)
    offset = local[:, None] - my_starts[None, :]
    inside = ((offset >= 0) & (offset < my_lengths[None, :])).astype(jnp.int32)
    source = jnp.sum(inside * (blocks * row_count + my_actor + offset), axis=1)
    chosen = []
    for step in ORDER:
        place = (p + step) % SIDE
        numbers = jnp.arange(SIDE, dtype=jnp.int32)
        block = jnp.where(c == 0, place * SIDE + numbers, numbers * SIDE + place)
        rows = (block[:, None] * row_count + local[None, :]).reshape(-1)
        chosen.append((source[:, None] == rows[None, :]).astype(jnp.bfloat16))

    actor_of = pair_index[0] // group_count
    block_of = pair_index[0] % group_count
    hit = (actor_of[:, None, None] == blocks[None, :, None]) & (
        block_of[:, None, None] == blocks[None, None, :]
    )
    length = jnp.sum(jnp.where(hit, counts[None], 0), axis=(1, 2))
    begin = actor_of * row_count + jnp.sum(jnp.where(hit, actor_start[None], 0), axis=(1, 2))
    offsets = jnp.arange(cap_size, dtype=jnp.int32)
    wanted = jnp.where(offsets[None, :] < length[:, None], begin[:, None] + offsets[None, :], -1)
    target_column = (slice_targets - grp * w_vocab.shape[1])[:, None]
    gains = [gain[None, :] for gain in (attn_gain, mlp_gain, final_gain)]
    key_cols, value_cols, cosine, sine, allowed, target_column, chosen, wanted, gains = (
        lax.optimization_barrier(
            (key_cols, value_cols, cosine, sine, allowed, target_column, chosen, wanted, gains)
        )
    )
    projected = project(attn_chunks, gains[0], (w_query, key_cols, value_cols))
    (context,) = call(
        attention_kernel,
        [((slice_rows, local_heads * HEAD_SIZE), bf16)],
        [],
        *projected,
        cosine,
        sine,
        allowed,
    )
    mid = project_out(gather_slices(context), w_out, line_rows)

    (hidden,) = call(
        hidden_kernel,
        [((slice_rows, w_gate.shape[1]), bf16)],
        [],
        *project(gather_chunks(mid), gains[1], (w_gate, w_up)),
    )
    final_chunks = gather_chunks(project_out(gather_slices(hidden), w_down, mid))
    (sums,) = call(
        score_kernel,
        [((8, 128), f32)],
        [],
        *project(final_chunks, gains[2], (w_vocab,)),
        target_column,
    )

    final_rows = 0.0
    for pattern, chunk in zip(chosen, final_chunks):
        final_rows = final_rows + jnp.dot(pattern, chunk, preferred_element_type=jnp.float32)
    final_rows = final_rows.astype(jnp.bfloat16)

    for send in (send_first, send_second):
        parts = [send(sums, step) for step in (1, 3, 2)]
        sums = sums + parts[0] + parts[1] + parts[2]
    slice_logp = sums[1:2, :slice_rows] - jnp.log(sums[0:1, :slice_rows])
    other = swap_cores(slice_logp)
    chip = jnp.concatenate(
        [jnp.where(c == 0, slice_logp, other), jnp.where(c == 0, other, slice_logp)], axis=1
    )
    got = [chip] + [send_y(chip, -step) for step in (1, 2, 3)]
    token_logp = jnp.concatenate(got, axis=1).reshape(-1)

    actual = (all_ids + y * (CORES * slice_rows)) % all_rows
    scores = jnp.sum(
        jnp.where(wanted.reshape(-1, 1) == actual[None, :], token_logp[None, :], 0.0), axis=1
    )
    return final_rows, scores.reshape(1, 2 * cap_size)


def solution(mesh):
    in_specs = (
        P("grp", "tp"),
        P(),
        P(),
        P(("grp", "tp"), None),
        P("tp"),
        P("tp", "grp"),
        P("tp", None),
        P("tp", None),
        P("grp", "tp"),
        P("tp"),
        P("tp", "grp"),
        P("tp", "grp"),
        P("grp", "tp"),
        P("tp"),
        P("tp", "grp"),
    )
    out_specs = (P("grp", "tp"), P(("grp", "tp"), None))
    return jax.shard_map(
        per_device, mesh=mesh, in_specs=in_specs, out_specs=out_specs, check_vma=False
    )
```

```python
import functools
import math

import jax
import jax.numpy as jnp
from jax import lax
from jax.experimental import pallas as pl
from jax.experimental.pallas import tpu as pltpu
from jax.sharding import PartitionSpec as P

MODEL_WIDTH = 12288
QUERY_HEADS = 96
KEY_VALUE_HEADS = 8
HEAD_SIZE = 128
SIDE = 4
CORES = 2
STARTS = (2, 1, 3)
ORDER = (0,) + STARTS


def coords(device):
    grp, tp = divmod(device, SIDE * CORES)
    return grp // SIDE, grp % SIDE, tp // CORES, tp % CORES


def permute(value, place):
    pairs = []
    for device in range(SIDE * SIDE * SIDE * CORES):
        x, z, y, c = place(*coords(device))
        target = ((x % SIDE) * SIDE + z % SIDE) * SIDE * CORES + (y % SIDE) * CORES + c
        pairs.append((device, target))
    return lax.ppermute(value, ("grp", "tp"), pairs)


def send_first(value, step):
    return permute(
        value, lambda x, z, y, c: (x + step, z, y, c) if c == 0 else (x, z + step, y, c)
    )


def send_second(value, step):
    return permute(
        value, lambda x, z, y, c: (x, z + step, y, c) if c == 0 else (x + step, z, y, c)
    )


def exchange_second(value, partner):
    return permute(
        value, lambda x, z, y, c: (x, partner(z), y, c) if c == 0 else (partner(x), z, y, c)
    )


def send_y(value, step):
    return permute(value, lambda x, z, y, c: (x, z, y + step, c))


def swap_cores(value):
    return permute(value, lambda x, z, y, c: (x, z, y, 1 - c))


def call(kernel, outs, scratch, *operands, places=None, after=None, limit=24):
    places = places or [pltpu.VMEM] * len(operands)
    body, count = kernel, len(operands)
    if after is not None:
        operands, places = operands + (after,), places + [pl.ANY]

        def body(*refs):
            kernel(*refs[:count], *refs[count + 1 :])

    return pl.pallas_call(
        body,
        out_shape=[jax.ShapeDtypeStruct(shape, dtype) for shape, dtype in outs],
        in_specs=[pl.BlockSpec(memory_space=place) for place in places],
        out_specs=[pl.BlockSpec(memory_space=pltpu.VMEM) for _ in outs],
        scratch_shapes=scratch,
        compiler_params=pltpu.CompilerParams(vmem_limit_bytes=limit * 1024 * 1024),
    )(*operands)


def pack_squares(squares):
    lane = lax.broadcasted_iota(jnp.int32, (squares.shape[0], 128), 1)
    high = squares.astype(jnp.bfloat16).astype(jnp.float32)
    tile = jnp.where(lane == 0, high, jnp.where(lane == 1, squares - high, 0.0))
    return tile.astype(jnp.bfloat16)


def order_kernel(where, first, second, third, fourth, chunk):
    rows = first.shape[0]
    for step, part in zip(ORDER, (first, second, third, fourth)):
        at = pl.multiple_of(lax.rem(where[1] + step, SIDE) * rows, rows)
        chunk[pl.ds(at, rows), :] = part[...]


def block_place(where, step, number):
    p, y, c = where[0], where[2], where[3]
    chunk = lax.rem(p + step, SIDE)
    x = jnp.where(c == 0, chunk, number)
    z = jnp.where(c == 0, number, chunk)
    return lax.rem(x + SIDE - y, SIDE), z // CORES, lax.rem(z, CORES)


def products(chunk, gain, matrices, out):
    wide = chunk[...].astype(jnp.float32)
    scaled = (wide * gain[...]).astype(jnp.bfloat16)
    start = 0
    for matrix in matrices:
        width = matrix.shape[1]
        for at in range(0, width, 256):
            size = min(256, width - at)
            out[:, start + at : start + at + size] = jnp.dot(
                scaled, matrix[:, at : at + size], preferred_element_type=jnp.float32
            ).astype(out.dtype)
        start += width
    out[:, start:] = pack_squares(jnp.sum(wide * wide, axis=1, keepdims=True))


def project_kernel(chunk, gain, *refs):
    products(chunk, gain, refs[:-1], refs[-1])


def project_last_kernel(order, where, *refs):
    earlier, chunk, gain, matrices = refs[:3], refs[3], refs[4], refs[5:-3]
    mine, other, last = refs[-3:]
    products(chunk, gain, matrices, last)
    rows = mine.shape[1] // CORES
    c = where[3]
    for step, part in zip(order, earlier + (last,)):
        for number in range(SIDE):
            slot, half, place = block_place(where, step, number)
            at = pl.multiple_of(place * rows, rows)
            block = part[number * rows : (number + 1) * rows, :]

            @pl.when(half == c)
            def _():
                mine[slot, pl.ds(at, rows), :] = block

            @pl.when(half != c)
            def _():
                other[slot, pl.ds(at, rows), :] = block


def pair_kernel(mine, other, own, *sent):
    width = mine.shape[2] - 128
    for step, out in enumerate((own,) + sent):
        left = mine[step].astype(jnp.float32)
        right = other[step].astype(jnp.float32)
        total = left + right
        out[:, :width] = total[:, :width].astype(out.dtype)
        squares = jnp.sum(total[:, width:], axis=1, keepdims=True)
        out[:, width:] = pack_squares(squares).astype(out.dtype)


def normed_sum(own, parts):
    width = own.shape[1] - 128
    total = own[...]
    for part in parts:
        total = total + part[...].astype(jnp.float32)
    squares = jnp.sum(total[:, width:], axis=1, keepdims=True)
    return total[:, :width] * lax.rsqrt(squares / MODEL_WIDTH + 1e-05)


def attention_kernel(own, first, second, third, cosine, sine, allowed, context):
    projected = normed_sum(own, (first, second, third))
    cosine, sine, allowed = cosine[...], sine[...], allowed[...]
    half = HEAD_SIZE // 2

    def rotate(vectors):
        turned = jnp.concatenate([vectors[:, half:], vectors[:, :half]], axis=1)
        return (vectors * cosine + turned * sine).astype(jnp.bfloat16)

    key_at = context.shape[1]
    key = rotate(projected[:, key_at : key_at + HEAD_SIZE])
    value = projected[:, key_at + HEAD_SIZE :].astype(jnp.bfloat16)
    for at in range(0, key_at, HEAD_SIZE):
        query = rotate(projected[:, at : at + HEAD_SIZE])
        scores = lax.dot_general(
            query, key, (((1,), (1,)), ((), ())), preferred_element_type=jnp.float32
        ) * (1.0 / math.sqrt(HEAD_SIZE))
        weights = jnp.where(allowed > 0.0, jnp.exp(scores), 0.0)
        probs = (weights / jnp.sum(weights, axis=1, keepdims=True)).astype(jnp.bfloat16)
        context[:, at : at + HEAD_SIZE] = jnp.dot(
            probs, value, preferred_element_type=jnp.float32
        ).astype(jnp.bfloat16)


def hidden_kernel(own, first, second, third, hidden):
    both = normed_sum(own, (first, second, third))
    width = hidden.shape[1]
    gate, up = both[:, :width], both[:, width:]
    hidden[...] = (gate / (1.0 + jnp.exp(-gate)) * up).astype(jnp.bfloat16)


def score_kernel(own, first, second, third, target, sums):
    logits = normed_sum(own, (first, second, third))
    rows = logits.shape[0]
    columns = lax.broadcasted_iota(jnp.int32, logits.shape, 1)
    totals = jnp.sum(jnp.exp(logits), axis=1, keepdims=True)
    chosen = jnp.sum(jnp.where(columns == target[...], logits, 0.0), axis=1, keepdims=True)
    line = lax.broadcasted_iota(jnp.int32, (rows, 128), 0)
    lane = lax.broadcasted_iota(jnp.int32, (rows, 128), 1)
    sums[...] = jnp.zeros_like(sums)
    sums[0:1, :] = jnp.sum(jnp.where(line == lane, totals, 0.0), axis=0, keepdims=True)
    sums[1:2, :] = jnp.sum(jnp.where(line == lane, chosen, 0.0), axis=0, keepdims=True)


def project_out_kernel(order, where, *refs):
    mine, theirs, matrix, outs, rows = refs[:4], refs[4:8], refs[8], refs[9:-1], refs[-1]
    c = where[3]
    size = mine[0].shape[0] // CORES
    lines = outs[0].shape[0]
    p, y = where[0], where[2]
    for index, chip in enumerate(ORDER):
        for whose, half in ((mine, c), (theirs, 1 - c)):
            for place in range(CORES):
                x, z = lax.rem(y + chip, SIDE), half * CORES + place
                chunk, number = jnp.where(c == 0, x, z), jnp.where(c == 0, z, x)
                step = lax.rem(chunk + SIDE - p, SIDE)
                position = sum(jnp.where(step == other, at, 0) for at, other in enumerate(order))
                to = pl.multiple_of(position * lines + number * size, size)
                rows[pl.ds(to, size), :] = whose[index][place * size : (place + 1) * size, :]

    tile = min(256, matrix.shape[1])
    for at in range(0, matrix.shape[1], tile):
        product = jnp.dot(
            rows[...], matrix[:, at : at + tile], preferred_element_type=jnp.float32
        )
        for position, out in enumerate(outs):
            out[:, at : at + tile] = product[position * lines : (position + 1) * lines].astype(
                out.dtype
            )


def sum_kernel(own, first, second, third, *halves):
    width = halves[0].shape[1]
    for number, out in enumerate(halves):
        at = slice(number * width, (number + 1) * width)
        total = own[:, at]
        for part in (first, second, third):
            total = total + part[:, at].astype(jnp.float32)
        out[...] = total.astype(out.dtype)


def add_kernel(left, left_got, right, right_got, left_out, right_out):
    for own, got, out in ((left, left_got, left_out), (right, right_got, right_out)):
        out[...] = (own[...].astype(jnp.float32) + got[...].astype(jnp.float32)).astype(out.dtype)


def residual_kernel(rows, left, left_got, right, right_got, out):
    width = left.shape[1]
    for number, (own, got) in enumerate(((left, left_got), (right, right_got))):
        at = slice(number * width, (number + 1) * width)
        change = own[...].astype(jnp.float32) + got[...].astype(jnp.float32)
        out[:, at] = (rows[:, at].astype(jnp.float32) + change).astype(out.dtype)


def per_device(
    actor_rows,
    route_counts,
    targets,
    pair_index,
    attn_gain,
    w_query,
    key_weight,
    value_weight,
    w_out,
    mlp_gain,
    w_gate,
    w_up,
    w_down,
    final_gain,
    w_vocab,
):
    grp = lax.axis_index("grp")
    tp = lax.axis_index("tp")
    x, z, y, c = grp // SIDE, grp % SIDE, tp // CORES, tp % CORES
    p = jnp.where(c == 0, x, z)
    q = jnp.where(c == 0, z, x)
    group_count = route_counts.shape[0]
    row_count, feat_width = actor_rows.shape
    all_rows = row_count * group_count
    slice_rows = all_rows // (SIDE * CORES)
    cap_size = 2 * row_count // group_count

    where = jnp.stack([p, q, y, c]).astype(jnp.int32)
    bf16, f32 = jnp.bfloat16, jnp.float32
    in_smem = [pltpu.SMEM]
    in_vmem = [pltpu.VMEM]
    sent_bf16 = [bf16] * (SIDE - 1)

    def line_chunk(block):
        got = [send_second(block, -step) for step in STARTS]
        (chunk,) = call(
            order_kernel,
            [((SIDE * row_count, feat_width), bf16)],
            [],
            where,
            block,
            *got,
            places=in_smem + in_vmem * SIDE,
        )
        return chunk

    def gather_chunks(chunk):
        return [chunk] + [send_first(chunk, -step) for step in STARTS]

    def project(chunks, gain, matrices):
        total = sum(matrix.shape[1] for matrix in matrices) + 128
        parts = []
        for chunk in chunks[:-1]:
            (part,) = call(
                project_kernel,
                [((chunk.shape[0], total), bf16)],
                [],
                chunk,
                gain,
                *matrices,
                after=parts[-1] if parts else None,
            )
            parts.append(part)
        halves = (SIDE, slice_rows, total)
        mine, other = call(
            functools.partial(project_last_kernel, ORDER),
            [(halves, bf16), (halves, bf16)],
            [pltpu.VMEM((chunks[-1].shape[0], total), bf16)],
            where,
            *parts,
            chunks[-1],
            gain,
            *matrices,
            places=in_smem + in_vmem * (SIDE + 1 + len(matrices)),
        )
        own, *sent = call(
            pair_kernel,
            [((slice_rows, total), kind) for kind in [f32] + sent_bf16],
            [],
            mine,
            swap_cores(other),
        )
        return [own] + [send_y(sent[step - 1], step) for step in STARTS]

    def gather_slices(block):
        mine = [block] + [send_y(block, -step) for step in STARTS]
        return mine + [swap_cores(part) for part in mine]

    def project_out(blocks, matrix, rows):
        wide = matrix.shape[1]
        order = STARTS + (0,)
        lines = SIDE * row_count
        parts = call(
            functools.partial(project_out_kernel, order),
            [((lines, wide), bf16 if step else f32) for step in order],
            [pltpu.VMEM((all_rows, matrix.shape[0]), bf16)],
            where,
            *blocks,
            matrix,
            places=in_smem + in_vmem * (len(blocks) + 1),
        )
        parts = [send_first(part, step) if step else part for part, step in zip(parts, order)]
        half = ((SIDE * row_count, wide // 2), bf16)
        left, right = call(sum_kernel, [half, half], [], parts[-1], *parts[:-1])
        near, far = (lambda i: i ^ 1), (lambda i: SIDE - 1 - i)
        left, right = call(
            add_kernel,
            [half, half],
            [],
            left,
            exchange_second(left, near),
            right,
            exchange_second(right, far),
        )
        (result,) = call(
            residual_kernel,
            [(rows.shape, bf16)],
            [],
            rows,
            left,
            exchange_second(left, far),
            right,
            exchange_second(right, near),
        )
        return result

    counts = route_counts
    actor_start = jnp.cumsum(counts, axis=1) - counts
    ref_start = jnp.cumsum(counts, axis=0) - counts
    blocks = jnp.arange(group_count, dtype=jnp.int32)
    local = jnp.arange(row_count, dtype=jnp.int32)

    def slice_tables(counts, actor_start, ref_start):
        row = jnp.arange(slice_rows, dtype=jnp.int32)[:, None]
        later = row >= row_count

        def spread(table):
            both = lax.dynamic_slice_in_dim(table, tp * CORES, CORES, 0)
            return jnp.where(later, both[1:2], both[0:1])

        offset = row - jnp.where(later, row_count, 0) - spread(actor_start)
        inside = (offset >= 0) & (offset < spread(counts))
        piece = jnp.where(later, group_count, 0) + blocks[None, :]

        def chosen(values):
            return jnp.sum(jnp.where(inside, values, 0), axis=1, keepdims=True)

        return (
            chosen(offset),
            chosen(piece),
            chosen(blocks[None, :] * row_count + spread(ref_start) + offset),
        )

    all_ids = jnp.arange(all_rows, dtype=jnp.int32)
    line_rows = line_chunk(actor_rows)

    local_heads = w_query.shape[1] // HEAD_SIZE
    key_value_head = grp * local_heads // (QUERY_HEADS // KEY_VALUE_HEADS)
    key_cols = lax.dynamic_slice_in_dim(key_weight, key_value_head * HEAD_SIZE, HEAD_SIZE, 1)
    value_cols = lax.dynamic_slice_in_dim(value_weight, key_value_head * HEAD_SIZE, HEAD_SIZE, 1)
    line_rows, counts, actor_start, ref_start, pair_index, gains = lax.optimization_barrier(
        (line_rows, counts, actor_start, ref_start, pair_index, (attn_gain, mlp_gain, final_gain))
    )
    position, sequence, ref_row = slice_tables(counts, actor_start, ref_start)
    attn_chunks = gather_chunks(line_rows)
    slice_targets = jnp.sum(
        jnp.where(ref_row == all_ids[None, :], targets[None, :], 0), axis=1
    )
    my_starts = lax.dynamic_index_in_dim(ref_start, grp, 1, keepdims=False)
    my_lengths = lax.dynamic_index_in_dim(counts, grp, 1, keepdims=False)
    my_actor = lax.dynamic_index_in_dim(actor_start, grp, 1, keepdims=False)
    offset = local[:, None] - my_starts[None, :]
    inside = ((offset >= 0) & (offset < my_lengths[None, :])).astype(jnp.int32)
    source = jnp.sum(inside * (blocks * row_count + my_actor + offset), axis=1)
    lane = jnp.arange(SIDE * row_count, dtype=jnp.int32)
    in_block = sum((lane >= number * row_count).astype(jnp.int32) for number in range(1, SIDE))
    chosen = []
    for step in ORDER:
        place = (p + step) % SIDE
        rows = jnp.where(
            c == 0,
            place * (SIDE * row_count) + lane,
            lane + in_block * ((SIDE - 1) * row_count) + place * row_count,
        )
        chosen.append((source[:, None] == rows[None, :]).astype(jnp.bfloat16))

    actor_of = pair_index[0] // group_count
    block_of = pair_index[0] % group_count
    hit = (actor_of[:, None, None] == blocks[None, :, None]) & (
        block_of[:, None, None] == blocks[None, None, :]
    )
    length = jnp.sum(jnp.where(hit, counts[None], 0), axis=(1, 2))
    begin = actor_of * row_count + jnp.sum(jnp.where(hit, actor_start[None], 0), axis=(1, 2))
    offsets = jnp.arange(cap_size, dtype=jnp.int32)
    wanted = jnp.where(offsets[None, :] < length[:, None], begin[:, None] + offsets[None, :], -1)
    chip_rows = jnp.arange(CORES * slice_rows, dtype=jnp.int32)
    actual = jnp.concatenate([(y + step) % SIDE * (CORES * slice_rows) + chip_rows for step in ORDER])
    wanted = wanted.reshape(-1, 1) == actual[None, :]
    exponent = jnp.arange(HEAD_SIZE // 2, dtype=jnp.float32) * (-2.0 / HEAD_SIZE)
    frequency = jnp.power(jnp.float32(1000000.0), exponent)
    angle = position.astype(jnp.float32) * frequency[None, :]
    cosine, sine = jnp.cos(angle), jnp.sin(angle)
    ids = jnp.arange(slice_rows, dtype=jnp.int32)
    allowed = (
        (sequence == sequence.T) & (ids[:, None] >= ids[None, :])
    ).astype(jnp.float32)
    cosine = jnp.concatenate([cosine, cosine], axis=1)
    sine = jnp.concatenate([-sine, sine], axis=1)
    target_column = (slice_targets - grp * w_vocab.shape[1])[:, None]
    gains = [gain[None, :] for gain in gains]
    key_cols, value_cols, cosine, sine, allowed, target_column, chosen, wanted, gains = (
        lax.optimization_barrier(
            (key_cols, value_cols, cosine, sine, allowed, target_column, chosen, wanted, gains)
        )
    )
    projected = project(attn_chunks, gains[0], (w_query, key_cols, value_cols))
    (context,) = call(
        attention_kernel,
        [((slice_rows, local_heads * HEAD_SIZE), bf16)],
        [],
        *projected,
        cosine,
        sine,
        allowed,
    )
    mid = project_out(gather_slices(context), w_out, line_rows)

    (hidden,) = call(
        hidden_kernel,
        [((slice_rows, w_gate.shape[1]), bf16)],
        [],
        *project(gather_chunks(mid), gains[1], (w_gate, w_up)),
    )
    final_chunks = gather_chunks(project_out(gather_slices(hidden), w_down, mid))
    (sums,) = call(
        score_kernel,
        [((8, 128), f32)],
        [],
        *project(final_chunks, gains[2], (w_vocab,)),
        target_column,
    )

    final_rows = 0.0
    for pattern, chunk in zip(chosen, final_chunks):
        final_rows = final_rows + jnp.dot(pattern, chunk, preferred_element_type=jnp.float32)
    final_rows = final_rows.astype(jnp.bfloat16)

    for send in (send_first, send_second):
        parts = [send(sums, step) for step in STARTS]
        sums = sums + parts[0] + parts[1] + parts[2]
    slice_logp = sums[1:2, :slice_rows] - jnp.log(sums[0:1, :slice_rows])
    other = swap_cores(slice_logp)
    chip = jnp.concatenate(
        [jnp.where(c == 0, slice_logp, other), jnp.where(c == 0, other, slice_logp)], axis=1
    )
    got = [chip] + [send_y(chip, -step) for step in STARTS]
    token_logp = jnp.concatenate(got, axis=1).reshape(-1)

    scores = jnp.sum(jnp.where(wanted, token_logp[None, :], 0.0), axis=1)
    return final_rows, scores.reshape(1, 2 * cap_size)


def solution(mesh):
    in_specs = (
        P("grp", "tp"),
        P(),
        P(),
        P(("grp", "tp"), None),
        P("tp"),
        P("tp", "grp"),
        P("tp", None),
        P("tp", None),
        P("grp", "tp"),
        P("tp"),
        P("tp", "grp"),
        P("tp", "grp"),
        P("grp", "tp"),
        P("tp"),
        P("tp", "grp"),
    )
    out_specs = (P("grp", "tp"), P(("grp", "tp"), None))
    return jax.shard_map(
        per_device, mesh=mesh, in_specs=in_specs, out_specs=out_specs, check_vma=False
    )
```

```python
import functools
import math

import jax
import jax.numpy as jnp
from jax import lax
from jax.experimental import pallas as pl
from jax.experimental.pallas import tpu as pltpu
from jax.sharding import PartitionSpec as P

MODEL_WIDTH = 12288
QUERY_HEADS = 96
KEY_VALUE_HEADS = 8
HEAD_SIZE = 128
SIDE = 4
CORES = 2
STARTS = (2, 1, 3)
ORDER = (0,) + STARTS


def coords(device):
    grp, tp = divmod(device, SIDE * CORES)
    return grp // SIDE, grp % SIDE, tp // CORES, tp % CORES


def permute(value, place):
    pairs = []
    for device in range(SIDE * SIDE * SIDE * CORES):
        x, z, y, c = place(*coords(device))
        target = ((x % SIDE) * SIDE + z % SIDE) * SIDE * CORES + (y % SIDE) * CORES + c
        pairs.append((device, target))
    return lax.ppermute(value, ("grp", "tp"), pairs)


def send_first(value, step):
    return permute(
        value, lambda x, z, y, c: (x + step, z, y, c) if c == 0 else (x, z + step, y, c)
    )


def send_second(value, step):
    return permute(
        value, lambda x, z, y, c: (x, z + step, y, c) if c == 0 else (x + step, z, y, c)
    )


def exchange_second(value, partner):
    return permute(
        value, lambda x, z, y, c: (x, partner(z), y, c) if c == 0 else (partner(x), z, y, c)
    )


def send_y(value, step):
    return permute(value, lambda x, z, y, c: (x, z, y + step, c))


def swap_cores(value):
    return permute(value, lambda x, z, y, c: (x, z, y, 1 - c))


def call(kernel, outs, scratch, *operands, places=None, after=None, limit=24):
    places = places or [pltpu.VMEM] * len(operands)
    body, count = kernel, len(operands)
    if after is not None:
        operands, places = operands + (after,), places + [pl.ANY]

        def body(*refs):
            kernel(*refs[:count], *refs[count + 1 :])

    return pl.pallas_call(
        body,
        out_shape=[jax.ShapeDtypeStruct(shape, dtype) for shape, dtype in outs],
        in_specs=[pl.BlockSpec(memory_space=place) for place in places],
        out_specs=[pl.BlockSpec(memory_space=pltpu.VMEM) for _ in outs],
        scratch_shapes=scratch,
        compiler_params=pltpu.CompilerParams(vmem_limit_bytes=limit * 1024 * 1024),
    )(*operands)


def pack_squares(squares):
    lane = lax.broadcasted_iota(jnp.int32, (squares.shape[0], 128), 1)
    high = squares.astype(jnp.bfloat16).astype(jnp.float32)
    tile = jnp.where(lane == 0, high, jnp.where(lane == 1, squares - high, 0.0))
    return tile.astype(jnp.bfloat16)


def order_kernel(where, first, second, third, fourth, chunk):
    rows = first.shape[0]
    for step, part in zip(ORDER, (first, second, third, fourth)):
        at = pl.multiple_of(lax.rem(where[1] + step, SIDE) * rows, rows)
        chunk[pl.ds(at, rows), :] = part[...]


def block_place(where, step, number):
    p, y, c = where[0], where[2], where[3]
    chunk = lax.rem(p + step, SIDE)
    x = jnp.where(c == 0, chunk, number)
    z = jnp.where(c == 0, number, chunk)
    return lax.rem(x + SIDE - y, SIDE), z // CORES, lax.rem(z, CORES)


def products(chunk, gain, matrices, out):
    wide = chunk[...].astype(jnp.float32)
    scaled = (wide * gain[...]).astype(jnp.bfloat16)
    start = 0
    for matrix in matrices:
        width = matrix.shape[1]
        for at in range(0, width, 256):
            size = min(256, width - at)
            out[:, start + at : start + at + size] = jnp.dot(
                scaled, matrix[:, at : at + size], preferred_element_type=jnp.float32
            ).astype(out.dtype)
        start += width
    out[:, start:] = pack_squares(jnp.sum(wide * wide, axis=1, keepdims=True))


def project_kernel(chunk, gain, *refs):
    products(chunk, gain, refs[:-1], refs[-1])


def project_last_kernel(order, where, *refs):
    earlier, chunk, gain, matrices = refs[:3], refs[3], refs[4], refs[5:-3]
    mine, other, last = refs[-3:]
    products(chunk, gain, matrices, last)
    rows = mine.shape[1] // CORES
    c = where[3]
    for step, part in zip(order, earlier + (last,)):
        for number in range(SIDE):
            slot, half, place = block_place(where, step, number)
            at = pl.multiple_of(place * rows, rows)
            block = part[number * rows : (number + 1) * rows, :]

            @pl.when(half == c)
            def _():
                mine[slot, pl.ds(at, rows), :] = block

            @pl.when(half != c)
            def _():
                other[slot, pl.ds(at, rows), :] = block


def pair_kernel(mine, other, own, *sent):
    width = mine.shape[2] - 128
    for step, out in enumerate((own,) + sent):
        left = mine[step].astype(jnp.float32)
        right = other[step].astype(jnp.float32)
        total = left + right
        out[:, :width] = total[:, :width].astype(out.dtype)
        squares = jnp.sum(total[:, width:], axis=1, keepdims=True)
        out[:, width:] = pack_squares(squares).astype(out.dtype)


def normed_sum(own, parts):
    width = own.shape[1] - 128
    total = own[...]
    for part in parts:
        total = total + part[...].astype(jnp.float32)
    squares = jnp.sum(total[:, width:], axis=1, keepdims=True)
    return total[:, :width] * lax.rsqrt(squares / MODEL_WIDTH + 1e-05)


def attention_kernel(own, first, second, third, cosine, sine, allowed, context):
    projected = normed_sum(own, (first, second, third))
    cosine, sine, allowed = cosine[...], sine[...], allowed[...]
    half = HEAD_SIZE // 2

    def rotate(vectors):
        turned = jnp.concatenate([vectors[:, half:], vectors[:, :half]], axis=1)
        return (vectors * cosine + turned * sine).astype(jnp.bfloat16)

    key_at = context.shape[1]
    key = rotate(projected[:, key_at : key_at + HEAD_SIZE])
    value = projected[:, key_at + HEAD_SIZE :].astype(jnp.bfloat16)
    rows, heads = context.shape[0], key_at // HEAD_SIZE
    query = jnp.concatenate(
        [rotate(projected[:, at : at + HEAD_SIZE]) for at in range(0, key_at, HEAD_SIZE)], axis=0
    )
    scores = lax.dot_general(
        query, key, (((1,), (1,)), ((), ())), preferred_element_type=jnp.float32
    ) * (1.0 / math.sqrt(HEAD_SIZE))
    allowed = jnp.concatenate([allowed] * heads, axis=0)
    weights = jnp.where(allowed > 0.0, jnp.exp(scores), 0.0)
    probs = (weights / jnp.sum(weights, axis=1, keepdims=True)).astype(jnp.bfloat16)
    result = jnp.dot(probs, value, preferred_element_type=jnp.float32).astype(jnp.bfloat16)
    for head in range(heads):
        context[:, head * HEAD_SIZE : (head + 1) * HEAD_SIZE] = result[
            head * rows : (head + 1) * rows
        ]


def hidden_kernel(own, first, second, third, hidden):
    both = normed_sum(own, (first, second, third))
    width = hidden.shape[1]
    gate, up = both[:, :width], both[:, width:]
    hidden[...] = (gate / (1.0 + jnp.exp(-gate)) * up).astype(jnp.bfloat16)


def score_kernel(own, first, second, third, target, sums):
    logits = normed_sum(own, (first, second, third))
    rows = logits.shape[0]
    columns = lax.broadcasted_iota(jnp.int32, logits.shape, 1)
    totals = jnp.sum(jnp.exp(logits), axis=1, keepdims=True)
    chosen = jnp.sum(jnp.where(columns == target[...], logits, 0.0), axis=1, keepdims=True)
    line = lax.broadcasted_iota(jnp.int32, (rows, 128), 0)
    lane = lax.broadcasted_iota(jnp.int32, (rows, 128), 1)
    sums[...] = jnp.zeros_like(sums)
    sums[0:1, :] = jnp.sum(jnp.where(line == lane, totals, 0.0), axis=0, keepdims=True)
    sums[1:2, :] = jnp.sum(jnp.where(line == lane, chosen, 0.0), axis=0, keepdims=True)


def project_out_kernel(order, where, *refs):
    mine, theirs, matrix, outs, rows = refs[:4], refs[4:8], refs[8], refs[9:-1], refs[-1]
    c = where[3]
    size = mine[0].shape[0] // CORES
    lines = outs[0].shape[0]
    p, y = where[0], where[2]
    every = order + tuple(step for step in ORDER if step not in order)
    for index, chip in enumerate(ORDER):
        for whose, half in ((mine, c), (theirs, 1 - c)):
            for place in range(CORES):
                x, z = lax.rem(y + chip, SIDE), half * CORES + place
                chunk, number = jnp.where(c == 0, x, z), jnp.where(c == 0, z, x)
                step = lax.rem(chunk + SIDE - p, SIDE)
                position = sum(
                    jnp.where(step == other, at, 0) for at, other in enumerate(every)
                )
                to = pl.multiple_of(position * lines + number * size, size)
                rows[pl.ds(to, size), :] = whose[index][place * size : (place + 1) * size, :]

    tile = min(256, matrix.shape[1])
    for at in range(0, matrix.shape[1], tile):
        product = jnp.dot(
            rows[: len(order) * lines, :],
            matrix[:, at : at + tile],
            preferred_element_type=jnp.float32,
        )
        for position, out in enumerate(outs):
            out[:, at : at + tile] = product[position * lines : (position + 1) * lines].astype(
                out.dtype
            )


def sum_kernel(own, first, second, third, *halves):
    width = halves[0].shape[1]
    for number, out in enumerate(halves):
        at = slice(number * width, (number + 1) * width)
        total = own[:, at]
        for part in (first, second, third):
            total = total + part[:, at].astype(jnp.float32)
        out[...] = total.astype(out.dtype)


def add_kernel(left, left_got, right, right_got, left_out, right_out):
    for own, got, out in ((left, left_got, left_out), (right, right_got, right_out)):
        out[...] = (own[...].astype(jnp.float32) + got[...].astype(jnp.float32)).astype(out.dtype)


def residual_kernel(rows, left, left_got, right, right_got, out):
    width = left.shape[1]
    for number, (own, got) in enumerate(((left, left_got), (right, right_got))):
        at = slice(number * width, (number + 1) * width)
        change = own[...].astype(jnp.float32) + got[...].astype(jnp.float32)
        out[:, at] = (rows[:, at].astype(jnp.float32) + change).astype(out.dtype)


def per_device(
    actor_rows,
    route_counts,
    targets,
    pair_index,
    attn_gain,
    w_query,
    key_weight,
    value_weight,
    w_out,
    mlp_gain,
    w_gate,
    w_up,
    w_down,
    final_gain,
    w_vocab,
):
    grp = lax.axis_index("grp")
    tp = lax.axis_index("tp")
    x, z, y, c = grp // SIDE, grp % SIDE, tp // CORES, tp % CORES
    p = jnp.where(c == 0, x, z)
    q = jnp.where(c == 0, z, x)
    group_count = route_counts.shape[0]
    row_count, feat_width = actor_rows.shape
    all_rows = row_count * group_count
    slice_rows = all_rows // (SIDE * CORES)
    cap_size = 2 * row_count // group_count

    where = jnp.stack([p, q, y, c]).astype(jnp.int32)
    bf16, f32 = jnp.bfloat16, jnp.float32
    in_smem = [pltpu.SMEM]
    in_vmem = [pltpu.VMEM]
    sent_bf16 = [bf16] * (SIDE - 1)

    def line_chunk(block):
        got = [send_second(block, -step) for step in STARTS]
        (chunk,) = call(
            order_kernel,
            [((SIDE * row_count, feat_width), bf16)],
            [],
            where,
            block,
            *got,
            places=in_smem + in_vmem * SIDE,
        )
        return chunk

    def gather_chunks(chunk):
        return [chunk] + [send_first(chunk, -step) for step in STARTS]

    def project(chunks, gain, matrices):
        total = sum(matrix.shape[1] for matrix in matrices) + 128
        parts = []
        for chunk in chunks[:-1]:
            (part,) = call(
                project_kernel,
                [((chunk.shape[0], total), bf16)],
                [],
                chunk,
                gain,
                *matrices,
                after=parts[-1] if parts else None,
            )
            parts.append(part)
        halves = (SIDE, slice_rows, total)
        mine, other = call(
            functools.partial(project_last_kernel, ORDER),
            [(halves, bf16), (halves, bf16)],
            [pltpu.VMEM((chunks[-1].shape[0], total), bf16)],
            where,
            *parts,
            chunks[-1],
            gain,
            *matrices,
            places=in_smem + in_vmem * (SIDE + 1 + len(matrices)),
        )
        own, *sent = call(
            pair_kernel,
            [((slice_rows, total), kind) for kind in [f32] + sent_bf16],
            [],
            mine,
            swap_cores(other),
        )
        return [own] + [send_y(sent[step - 1], step) for step in STARTS]

    def gather_slices(block):
        mine = [block] + [send_y(block, -step) for step in STARTS]
        return mine + [swap_cores(part) for part in mine]

    def project_out(blocks, matrix, rows):
        wide = matrix.shape[1]
        lines = SIDE * row_count

        def products_of(order, kind, after):
            return call(
                functools.partial(project_out_kernel, order),
                [((lines, wide), kind)] * len(order),
                [pltpu.VMEM((all_rows, matrix.shape[0]), bf16)],
                where,
                *blocks,
                matrix,
                places=in_smem + in_vmem * (len(blocks) + 1),
                after=after,
            )

        parts = products_of(STARTS, bf16, None)
        (own,) = products_of((0,), f32, parts[-1])
        parts = [send_first(part, step) for part, step in zip(parts, STARTS)] + [own]
        half = ((SIDE * row_count, wide // 2), bf16)
        left, right = call(sum_kernel, [half, half], [], parts[-1], *parts[:-1])
        near, far = (lambda i: i ^ 1), (lambda i: SIDE - 1 - i)
        left, right = call(
            add_kernel,
            [half, half],
            [],
            left,
            exchange_second(left, near),
            right,
            exchange_second(right, far),
        )
        (result,) = call(
            residual_kernel,
            [(rows.shape, bf16)],
            [],
            rows,
            left,
            exchange_second(left, far),
            right,
            exchange_second(right, near),
        )
        return result

    counts = route_counts
    actor_start = jnp.cumsum(counts, axis=1) - counts
    ref_start = jnp.cumsum(counts, axis=0) - counts
    blocks = jnp.arange(group_count, dtype=jnp.int32)
    local = jnp.arange(row_count, dtype=jnp.int32)

    def slice_tables(counts, actor_start, ref_start):
        row = jnp.arange(slice_rows, dtype=jnp.int32)[:, None]
        later = row >= row_count

        def spread(table):
            both = lax.dynamic_slice_in_dim(table, tp * CORES, CORES, 0)
            return jnp.where(later, both[1:2], both[0:1])

        offset = row - jnp.where(later, row_count, 0) - spread(actor_start)
        inside = (offset >= 0) & (offset < spread(counts))
        piece = jnp.where(later, group_count, 0) + blocks[None, :]

        def chosen(values):
            return jnp.sum(jnp.where(inside, values, 0), axis=1, keepdims=True)

        return (
            chosen(offset),
            chosen(piece),
            chosen(blocks[None, :] * row_count + spread(ref_start) + offset),
        )

    all_ids = jnp.arange(all_rows, dtype=jnp.int32)
    line_rows = line_chunk(actor_rows)

    local_heads = w_query.shape[1] // HEAD_SIZE
    key_value_head = grp * local_heads // (QUERY_HEADS // KEY_VALUE_HEADS)
    key_cols = lax.dynamic_slice_in_dim(key_weight, key_value_head * HEAD_SIZE, HEAD_SIZE, 1)
    value_cols = lax.dynamic_slice_in_dim(value_weight, key_value_head * HEAD_SIZE, HEAD_SIZE, 1)
    line_rows, counts, actor_start, ref_start, pair_index, gains = lax.optimization_barrier(
        (line_rows, counts, actor_start, ref_start, pair_index, (attn_gain, mlp_gain, final_gain))
    )
    position, sequence, ref_row = slice_tables(counts, actor_start, ref_start)
    attn_chunks = gather_chunks(line_rows)
    slice_targets = jnp.sum(
        jnp.where(ref_row == all_ids[None, :], targets[None, :], 0), axis=1
    )
    my_starts = lax.dynamic_index_in_dim(ref_start, grp, 1, keepdims=False)
    my_lengths = lax.dynamic_index_in_dim(counts, grp, 1, keepdims=False)
    my_actor = lax.dynamic_index_in_dim(actor_start, grp, 1, keepdims=False)
    offset = local[:, None] - my_starts[None, :]
    inside = ((offset >= 0) & (offset < my_lengths[None, :])).astype(jnp.int32)
    source = jnp.sum(inside * (blocks * row_count + my_actor + offset), axis=1)
    lane = jnp.arange(SIDE * row_count, dtype=jnp.int32)
    in_block = sum((lane >= number * row_count).astype(jnp.int32) for number in range(1, SIDE))
    chosen = []
    for step in ORDER:
        place = (p + step) % SIDE
        rows = jnp.where(
            c == 0,
            place * (SIDE * row_count) + lane,
            lane + in_block * ((SIDE - 1) * row_count) + place * row_count,
        )
        chosen.append((source[:, None] == rows[None, :]).astype(jnp.bfloat16))

    entry = jnp.arange(2 * cap_size, dtype=jnp.int32)[:, None]
    second = entry >= cap_size
    offset = entry - jnp.where(second, cap_size, 0)
    piece = jnp.where(second, pair_index[0:1, 1:2], pair_index[0:1, 0:1])
    actor_of, block_of = piece // group_count, piece % group_count

    def of_piece(table):
        line = jnp.sum(
            jnp.where(actor_of[:, :, None] == blocks[None, :, None], table[None], 0), axis=1
        )
        return jnp.sum(jnp.where(block_of == blocks[None, :], line, 0), axis=1, keepdims=True)

    begin = actor_of * row_count + of_piece(actor_start)
    wanted = jnp.where(offset < of_piece(counts), begin + offset, -1)
    chip_rows = CORES * slice_rows
    at = sum((all_ids >= number * chip_rows).astype(jnp.int32) for number in range(1, SIDE))
    step = sum(jnp.where(at == number, ORDER[number], 0) for number in range(1, SIDE))
    actual = ((y + step) & (SIDE - 1)) * chip_rows + all_ids - at * chip_rows
    wanted = wanted == actual[None, :]
    exponent = jnp.arange(HEAD_SIZE // 2, dtype=jnp.float32) * (-2.0 / HEAD_SIZE)
    frequency = jnp.power(jnp.float32(1000000.0), exponent)
    angle = position.astype(jnp.float32) * frequency[None, :]
    cosine, sine = jnp.cos(angle), jnp.sin(angle)
    ids = jnp.arange(slice_rows, dtype=jnp.int32)
    allowed = (
        (sequence == sequence.T) & (ids[:, None] >= ids[None, :])
    ).astype(jnp.float32)
    cosine = jnp.concatenate([cosine, cosine], axis=1)
    sine = jnp.concatenate([-sine, sine], axis=1)
    target_column = (slice_targets - grp * w_vocab.shape[1])[:, None]
    key_cols, value_cols, cosine, sine, allowed, target_column, chosen, wanted, gains = (
        lax.optimization_barrier(
            (key_cols, value_cols, cosine, sine, allowed, target_column, chosen, wanted, gains)
        )
    )
    projected = project(attn_chunks, gains[0], (w_query, key_cols, value_cols))
    (context,) = call(
        attention_kernel,
        [((slice_rows, local_heads * HEAD_SIZE), bf16)],
        [],
        *projected,
        cosine,
        sine,
        allowed,
    )
    mid = project_out(gather_slices(context), w_out, line_rows)

    (hidden,) = call(
        hidden_kernel,
        [((slice_rows, w_gate.shape[1]), bf16)],
        [],
        *project(gather_chunks(mid), gains[1], (w_gate, w_up)),
    )
    final_chunks = gather_chunks(project_out(gather_slices(hidden), w_down, mid))
    (sums,) = call(
        score_kernel,
        [((8, 128), f32)],
        [],
        *project(final_chunks, gains[2], (w_vocab,)),
        target_column,
    )

    final_rows = 0.0
    for pattern, chunk in zip(chosen, final_chunks):
        final_rows = final_rows + jnp.dot(pattern, chunk, preferred_element_type=jnp.float32)
    final_rows = final_rows.astype(jnp.bfloat16)

    for send in (send_first, send_second):
        parts = [send(sums, step) for step in STARTS]
        sums = sums + parts[0] + parts[1] + parts[2]
    slice_logp = sums[1:2, :slice_rows] - jnp.log(sums[0:1, :slice_rows])
    other = swap_cores(slice_logp)
    chip = jnp.concatenate(
        [jnp.where(c == 0, slice_logp, other), jnp.where(c == 0, other, slice_logp)], axis=1
    )
    got = [chip] + [send_y(chip, -step) for step in STARTS]
    token_logp = jnp.concatenate(got, axis=1).reshape(-1)

    scores = jnp.sum(jnp.where(wanted, token_logp[None, :], 0.0), axis=1)
    return final_rows, scores.reshape(1, 2 * cap_size)


def solution(mesh):
    in_specs = (
        P("grp", "tp"),
        P(),
        P(),
        P(("grp", "tp"), None),
        P("tp"),
        P("tp", "grp"),
        P("tp", None),
        P("tp", None),
        P("grp", "tp"),
        P("tp"),
        P("tp", "grp"),
        P("tp", "grp"),
        P("grp", "tp"),
        P("tp"),
        P("tp", "grp"),
    )
    out_specs = (P("grp", "tp"), P(("grp", "tp"), None))
    return jax.shard_map(
        per_device, mesh=mesh, in_specs=in_specs, out_specs=out_specs, check_vma=False
    )
```

```python
import functools
import math

import jax
import jax.numpy as jnp
from jax import lax
from jax.experimental import pallas as pl
from jax.experimental.pallas import tpu as pltpu
from jax.sharding import PartitionSpec as P

MODEL_WIDTH = 12288
QUERY_HEADS = 96
KEY_VALUE_HEADS = 8
HEAD_SIZE = 128
SIDE = 4
CORES = 2
STARTS = (2, 1, 3)
ORDER = (0,) + STARTS


def coords(device):
    grp, tp = divmod(device, SIDE * CORES)
    return grp // SIDE, grp % SIDE, tp // CORES, tp % CORES


def permute(value, place):
    pairs = []
    for device in range(SIDE * SIDE * SIDE * CORES):
        x, z, y, c = place(*coords(device))
        target = ((x % SIDE) * SIDE + z % SIDE) * SIDE * CORES + (y % SIDE) * CORES + c
        pairs.append((device, target))
    return lax.ppermute(value, ("grp", "tp"), pairs)


def send_first(value, step):
    return permute(
        value, lambda x, z, y, c: (x + step, z, y, c) if c == 0 else (x, z + step, y, c)
    )


def send_second(value, step):
    return permute(
        value, lambda x, z, y, c: (x, z + step, y, c) if c == 0 else (x + step, z, y, c)
    )


def exchange_second(value, partner):
    return permute(
        value, lambda x, z, y, c: (x, partner(z), y, c) if c == 0 else (partner(x), z, y, c)
    )


def send_y(value, step):
    return permute(value, lambda x, z, y, c: (x, z, y + step, c))


def swap_cores(value):
    return permute(value, lambda x, z, y, c: (x, z, y, 1 - c))


def call(kernel, outs, scratch, *operands, places=None, after=None, limit=24):
    places = places or [pltpu.VMEM] * len(operands)
    body, count = kernel, len(operands)
    if after is not None:
        operands, places = operands + (after,), places + [pl.ANY]

        def body(*refs):
            kernel(*refs[:count], *refs[count + 1 :])

    return pl.pallas_call(
        body,
        out_shape=[jax.ShapeDtypeStruct(shape, dtype) for shape, dtype in outs],
        in_specs=[pl.BlockSpec(memory_space=place) for place in places],
        out_specs=[pl.BlockSpec(memory_space=pltpu.VMEM) for _ in outs],
        scratch_shapes=scratch,
        compiler_params=pltpu.CompilerParams(vmem_limit_bytes=limit * 1024 * 1024),
    )(*operands)


def pack_squares(squares):
    lane = lax.broadcasted_iota(jnp.int32, (squares.shape[0], 128), 1)
    high = squares.astype(jnp.bfloat16).astype(jnp.float32)
    tile = jnp.where(lane == 0, high, jnp.where(lane == 1, squares - high, 0.0))
    return tile.astype(jnp.bfloat16)


def order_kernel(where, first, second, third, fourth, chunk):
    rows = first.shape[0]
    for step, part in zip(ORDER, (first, second, third, fourth)):
        at = pl.multiple_of(lax.rem(where[1] + step, SIDE) * rows, rows)
        chunk[pl.ds(at, rows), :] = part[...]


def block_place(where, step, number):
    p, y, c = where[0], where[2], where[3]
    chunk = lax.rem(p + step, SIDE)
    x = jnp.where(c == 0, chunk, number)
    z = jnp.where(c == 0, number, chunk)
    return lax.rem(x + SIDE - y, SIDE), z // CORES, lax.rem(z, CORES)


def products(chunk, gain, matrices, out):
    wide = chunk[...].astype(jnp.float32)
    scaled = (wide * gain[...]).astype(jnp.bfloat16)
    start = 0
    for matrix in matrices:
        width = matrix.shape[1]
        for at in range(0, width, 256):
            size = min(256, width - at)
            out[:, start + at : start + at + size] = jnp.dot(
                scaled, matrix[:, at : at + size], preferred_element_type=jnp.float32
            ).astype(out.dtype)
        start += width
    out[:, start:] = pack_squares(jnp.sum(wide * wide, axis=1, keepdims=True))


def project_kernel(chunk, gain, *refs):
    products(chunk, gain, refs[:-1], refs[-1])


def project_last_kernel(order, where, *refs):
    earlier, chunk, gain, matrices = refs[:3], refs[3], refs[4], refs[5:-3]
    mine, other, last = refs[-3:]
    products(chunk, gain, matrices, last)
    rows = mine.shape[1] // CORES
    c = where[3]
    for step, part in zip(order, earlier + (last,)):
        for number in range(SIDE):
            slot, half, place = block_place(where, step, number)
            at = pl.multiple_of(place * rows, rows)
            block = part[number * rows : (number + 1) * rows, :]

            @pl.when(half == c)
            def _():
                mine[slot, pl.ds(at, rows), :] = block

            @pl.when(half != c)
            def _():
                other[slot, pl.ds(at, rows), :] = block


def pair_kernel(mine, other, own, *sent):
    width = mine.shape[2] - 128
    for step, out in enumerate((own,) + sent):
        left = mine[step].astype(jnp.float32)
        right = other[step].astype(jnp.float32)
        total = left + right
        out[:, :width] = total[:, :width].astype(out.dtype)
        squares = jnp.sum(total[:, width:], axis=1, keepdims=True)
        out[:, width:] = pack_squares(squares).astype(out.dtype)


def normed_sum(own, parts):
    width = own.shape[1] - 128
    total = own[...]
    for part in parts:
        total = total + part[...].astype(jnp.float32)
    squares = jnp.sum(total[:, width:], axis=1, keepdims=True)
    return total[:, :width] * lax.rsqrt(squares / MODEL_WIDTH + 1e-05)


def attention_kernel(own, first, second, third, cosine, sine, allowed, context):
    projected = normed_sum(own, (first, second, third))
    cosine, sine, allowed = cosine[...], sine[...], allowed[...]
    half = HEAD_SIZE // 2

    def rotate(vectors):
        turned = jnp.concatenate([vectors[:, half:], vectors[:, :half]], axis=1)
        return (vectors * cosine + turned * sine).astype(jnp.bfloat16)

    key_at = context.shape[1]
    key = rotate(projected[:, key_at : key_at + HEAD_SIZE])
    value = projected[:, key_at + HEAD_SIZE :].astype(jnp.bfloat16)
    rows, heads = context.shape[0], key_at // HEAD_SIZE
    query = jnp.concatenate(
        [rotate(projected[:, at : at + HEAD_SIZE]) for at in range(0, key_at, HEAD_SIZE)], axis=0
    )
    scores = lax.dot_general(
        query, key, (((1,), (1,)), ((), ())), preferred_element_type=jnp.float32
    ) * (1.0 / math.sqrt(HEAD_SIZE))
    allowed = jnp.concatenate([allowed] * heads, axis=0)
    weights = jnp.where(allowed > 0.0, jnp.exp(scores), 0.0)
    probs = (weights / jnp.sum(weights, axis=1, keepdims=True)).astype(jnp.bfloat16)
    result = jnp.dot(probs, value, preferred_element_type=jnp.float32).astype(jnp.bfloat16)
    for head in range(heads):
        context[:, head * HEAD_SIZE : (head + 1) * HEAD_SIZE] = result[
            head * rows : (head + 1) * rows
        ]


def hidden_kernel(own, first, second, third, hidden):
    both = normed_sum(own, (first, second, third))
    width = hidden.shape[1]
    gate, up = both[:, :width], both[:, width:]
    hidden[...] = (gate / (1.0 + jnp.exp(-gate)) * up).astype(jnp.bfloat16)


def score_kernel(own, first, second, third, target, sums):
    logits = normed_sum(own, (first, second, third))
    rows = logits.shape[0]
    columns = lax.broadcasted_iota(jnp.int32, logits.shape, 1)
    totals = jnp.sum(jnp.exp(logits), axis=1, keepdims=True)
    chosen = jnp.sum(jnp.where(columns == target[...], logits, 0.0), axis=1, keepdims=True)
    line = lax.broadcasted_iota(jnp.int32, (rows, 128), 0)
    lane = lax.broadcasted_iota(jnp.int32, (rows, 128), 1)
    sums[...] = jnp.zeros_like(sums)
    sums[0:1, :] = jnp.sum(jnp.where(line == lane, totals, 0.0), axis=0, keepdims=True)
    sums[1:2, :] = jnp.sum(jnp.where(line == lane, chosen, 0.0), axis=0, keepdims=True)


def project_out_kernel(order, where, *refs):
    mine, theirs, matrix, outs, rows = refs[:4], refs[4:8], refs[8], refs[9:-1], refs[-1]
    c = where[3]
    size = mine[0].shape[0] // CORES
    lines = outs[0].shape[0]
    p, y = where[0], where[2]
    every = order + tuple(step for step in ORDER if step not in order)
    for index, chip in enumerate(ORDER):
        for whose, half in ((mine, c), (theirs, 1 - c)):
            for place in range(CORES):
                x, z = lax.rem(y + chip, SIDE), half * CORES + place
                chunk, number = jnp.where(c == 0, x, z), jnp.where(c == 0, z, x)
                step = lax.rem(chunk + SIDE - p, SIDE)
                position = sum(
                    jnp.where(step == other, at, 0) for at, other in enumerate(every)
                )
                to = pl.multiple_of(position * lines + number * size, size)
                rows[pl.ds(to, size), :] = whose[index][place * size : (place + 1) * size, :]

    tile = min(256, matrix.shape[1])
    for at in range(0, matrix.shape[1], tile):
        product = jnp.dot(
            rows[: len(order) * lines, :],
            matrix[:, at : at + tile],
            preferred_element_type=jnp.float32,
        )
        for position, out in enumerate(outs):
            out[:, at : at + tile] = product[position * lines : (position + 1) * lines].astype(
                out.dtype
            )


def sum_kernel(own, first, second, third, *halves):
    width = halves[0].shape[1]
    for number, out in enumerate(halves):
        at = slice(number * width, (number + 1) * width)
        total = own[:, at]
        for part in (first, second, third):
            total = total + part[:, at].astype(jnp.float32)
        out[...] = total.astype(out.dtype)


def add_kernel(left, left_got, right, right_got, left_out, right_out):
    for own, got, out in ((left, left_got, left_out), (right, right_got, right_out)):
        out[...] = (own[...].astype(jnp.float32) + got[...].astype(jnp.float32)).astype(out.dtype)


def residual_kernel(rows, left, left_got, right, right_got, out):
    width = left.shape[1]
    for number, (own, got) in enumerate(((left, left_got), (right, right_got))):
        at = slice(number * width, (number + 1) * width)
        change = own[...].astype(jnp.float32) + got[...].astype(jnp.float32)
        out[:, at] = (rows[:, at].astype(jnp.float32) + change).astype(out.dtype)


def per_device(
    actor_rows,
    route_counts,
    targets,
    pair_index,
    attn_gain,
    w_query,
    key_weight,
    value_weight,
    w_out,
    mlp_gain,
    w_gate,
    w_up,
    w_down,
    final_gain,
    w_vocab,
):
    grp = lax.axis_index("grp")
    tp = lax.axis_index("tp")
    x, z, y, c = grp // SIDE, grp % SIDE, tp // CORES, tp % CORES
    p = jnp.where(c == 0, x, z)
    q = jnp.where(c == 0, z, x)
    group_count = route_counts.shape[0]
    row_count, feat_width = actor_rows.shape
    all_rows = row_count * group_count
    slice_rows = all_rows // (SIDE * CORES)
    cap_size = 2 * row_count // group_count

    where = jnp.stack([p, q, y, c]).astype(jnp.int32)
    bf16, f32 = jnp.bfloat16, jnp.float32
    in_smem = [pltpu.SMEM]
    in_vmem = [pltpu.VMEM]
    sent_bf16 = [bf16] * (SIDE - 1)

    def line_chunk(block):
        got = [send_second(block, -step) for step in STARTS]
        (chunk,) = call(
            order_kernel,
            [((SIDE * row_count, feat_width), bf16)],
            [],
            where,
            block,
            *got,
            places=in_smem + in_vmem * SIDE,
        )
        return chunk

    def gather_chunks(chunk):
        return [chunk] + [send_first(chunk, -step) for step in STARTS]

    def project(chunks, gain, matrices):
        total = sum(matrix.shape[1] for matrix in matrices) + 128
        parts = []
        for chunk in chunks[:-1]:
            (part,) = call(
                project_kernel,
                [((chunk.shape[0], total), bf16)],
                [],
                chunk,
                gain,
                *matrices,
                after=parts[-1] if parts else None,
            )
            parts.append(part)
        halves = (SIDE, slice_rows, total)
        mine, other = call(
            functools.partial(project_last_kernel, ORDER),
            [(halves, bf16), (halves, bf16)],
            [pltpu.VMEM((chunks[-1].shape[0], total), bf16)],
            where,
            *parts,
            chunks[-1],
            gain,
            *matrices,
            places=in_smem + in_vmem * (SIDE + 1 + len(matrices)),
        )
        own, *sent = call(
            pair_kernel,
            [((slice_rows, total), kind) for kind in [f32] + sent_bf16],
            [],
            mine,
            swap_cores(other),
        )
        return [own] + [send_y(sent[step - 1], step) for step in STARTS]

    def gather_slices(block):
        mine = [block] + [send_y(block, -step) for step in STARTS]
        return mine + [swap_cores(part) for part in mine]

    def project_out(blocks, matrix, rows):
        wide = matrix.shape[1]
        lines = SIDE * row_count

        def products_of(order, kind, after):
            return call(
                functools.partial(project_out_kernel, order),
                [((lines, wide), kind)] * len(order),
                [pltpu.VMEM((all_rows, matrix.shape[0]), bf16)],
                where,
                *blocks,
                matrix,
                places=in_smem + in_vmem * (len(blocks) + 1),
                after=after,
            )

        parts = products_of(STARTS, bf16, None)
        (own,) = products_of((0,), f32, parts[-1])
        parts = [send_first(part, step) for part, step in zip(parts, STARTS)] + [own]
        half = ((SIDE * row_count, wide // 2), bf16)
        left, right = call(sum_kernel, [half, half], [], parts[-1], *parts[:-1])
        near, far = (lambda i: i ^ 1), (lambda i: SIDE - 1 - i)
        left, right = call(
            add_kernel,
            [half, half],
            [],
            left,
            exchange_second(left, near),
            right,
            exchange_second(right, far),
        )
        (result,) = call(
            residual_kernel,
            [(rows.shape, bf16)],
            [],
            rows,
            left,
            exchange_second(left, far),
            right,
            exchange_second(right, near),
        )
        return result

    counts = route_counts
    actor_start = jnp.cumsum(counts, axis=1) - counts
    ref_start = jnp.cumsum(counts, axis=0) - counts
    blocks = jnp.arange(group_count, dtype=jnp.int32)
    local = jnp.arange(row_count, dtype=jnp.int32)

    def slice_tables(counts, actor_start, ref_start):
        row = jnp.arange(slice_rows, dtype=jnp.int32)[:, None]
        later = row >= row_count

        def spread(table):
            both = lax.dynamic_slice_in_dim(table, tp * CORES, CORES, 0)
            return jnp.where(later, both[1:2], both[0:1])

        offset = row - jnp.where(later, row_count, 0) - spread(actor_start)
        inside = (offset >= 0) & (offset < spread(counts))
        piece = jnp.where(later, group_count, 0) + blocks[None, :]

        def chosen(values):
            return jnp.sum(jnp.where(inside, values, 0), axis=1, keepdims=True)

        return (
            chosen(offset),
            chosen(piece),
            chosen(blocks[None, :] * row_count + spread(ref_start) + offset),
        )

    all_ids = jnp.arange(all_rows, dtype=jnp.int32)
    line_rows = line_chunk(actor_rows)

    local_heads = w_query.shape[1] // HEAD_SIZE
    key_value_head = grp * local_heads // (QUERY_HEADS // KEY_VALUE_HEADS)
    key_cols = lax.dynamic_slice_in_dim(key_weight, key_value_head * HEAD_SIZE, HEAD_SIZE, 1)
    value_cols = lax.dynamic_slice_in_dim(value_weight, key_value_head * HEAD_SIZE, HEAD_SIZE, 1)
    line_rows, counts, actor_start, ref_start, pair_index, gains = lax.optimization_barrier(
        (line_rows, counts, actor_start, ref_start, pair_index, (attn_gain, mlp_gain, final_gain))
    )
    position, sequence, ref_row = slice_tables(counts, actor_start, ref_start)
    attn_chunks = gather_chunks(line_rows)
    slice_targets = jnp.sum(
        jnp.where(ref_row == all_ids[None, :], targets[None, :], 0), axis=1
    )
    my_starts = lax.dynamic_index_in_dim(ref_start, grp, 1, keepdims=False)
    my_lengths = lax.dynamic_index_in_dim(counts, grp, 1, keepdims=False)
    my_actor = lax.dynamic_index_in_dim(actor_start, grp, 1, keepdims=False)
    offset = local[:, None] - my_starts[None, :]
    inside = ((offset >= 0) & (offset < my_lengths[None, :])).astype(jnp.int32)
    source = jnp.sum(inside * (blocks * row_count + my_actor + offset), axis=1)
    lane = jnp.arange(SIDE * row_count, dtype=jnp.int32)
    in_block = sum((lane >= number * row_count).astype(jnp.int32) for number in range(1, SIDE))
    chosen = []
    for step in ORDER:
        place = (p + step) % SIDE
        rows = jnp.where(
            c == 0,
            place * (SIDE * row_count) + lane,
            lane + in_block * ((SIDE - 1) * row_count) + place * row_count,
        )
        chosen.append((source[:, None] == rows[None, :]).astype(jnp.bfloat16))

    entry = jnp.arange(2 * cap_size, dtype=jnp.int32)[:, None]
    second = entry >= cap_size
    offset = entry - jnp.where(second, cap_size, 0)
    piece = jnp.where(second, pair_index[0:1, 1:2], pair_index[0:1, 0:1])
    actor_of, block_of = piece // group_count, piece % group_count

    def of_piece(table):
        line = jnp.sum(
            jnp.where(actor_of[:, :, None] == blocks[None, :, None], table[None], 0), axis=1
        )
        return jnp.sum(jnp.where(block_of == blocks[None, :], line, 0), axis=1, keepdims=True)

    begin = actor_of * row_count + of_piece(actor_start)
    wanted = jnp.where(offset < of_piece(counts), begin + offset, -1)
    chip_rows = CORES * slice_rows
    at = sum((all_ids >= number * chip_rows).astype(jnp.int32) for number in range(1, SIDE))
    step = sum(jnp.where(at == number, ORDER[number], 0) for number in range(1, SIDE))
    actual = ((y + step) & (SIDE - 1)) * chip_rows + all_ids - at * chip_rows
    wanted = wanted == actual[None, :]
    exponent = jnp.arange(HEAD_SIZE // 2, dtype=jnp.float32) * (-2.0 / HEAD_SIZE)
    frequency = jnp.power(jnp.float32(1000000.0), exponent)
    angle = position.astype(jnp.float32) * frequency[None, :]
    cosine, sine = jnp.cos(angle), jnp.sin(angle)
    ids = jnp.arange(slice_rows, dtype=jnp.int32)
    allowed = (
        (sequence == sequence.T) & (ids[:, None] >= ids[None, :])
    ).astype(jnp.float32)
    cosine = jnp.concatenate([cosine, cosine], axis=1)
    sine = jnp.concatenate([-sine, sine], axis=1)
    target_column = (slice_targets - grp * w_vocab.shape[1])[:, None]
    key_cols, value_cols, cosine, sine, allowed, target_column, chosen, wanted, gains = (
        lax.optimization_barrier(
            (key_cols, value_cols, cosine, sine, allowed, target_column, chosen, wanted, gains)
        )
    )
    projected = project(attn_chunks, gains[0], (w_query, key_cols, value_cols))
    (context,) = call(
        attention_kernel,
        [((slice_rows, local_heads * HEAD_SIZE), bf16)],
        [],
        *projected,
        cosine,
        sine,
        allowed,
    )
    mid = project_out(gather_slices(context), w_out, line_rows)

    (hidden,) = call(
        hidden_kernel,
        [((slice_rows, w_gate.shape[1]), bf16)],
        [],
        *project(gather_chunks(mid), gains[1], (w_gate, w_up)),
    )
    final_chunks = gather_chunks(project_out(gather_slices(hidden), w_down, mid))
    (sums,) = call(
        score_kernel,
        [((8, 128), f32)],
        [],
        *project(final_chunks, gains[2], (w_vocab,)),
        target_column,
    )

    final_rows = 0.0
    for pattern, chunk in zip(chosen, final_chunks):
        final_rows = final_rows + jnp.dot(pattern, chunk, preferred_element_type=jnp.float32)
    final_rows = final_rows.astype(jnp.bfloat16)

    for send in (send_first, send_second):
        parts = [send(sums, step) for step in STARTS]
        sums = sums + parts[0] + parts[1] + parts[2]
    sums, final_rows = lax.optimization_barrier((sums, final_rows))
    slice_logp = sums[1:2, :slice_rows] - jnp.log(sums[0:1, :slice_rows])
    other = swap_cores(slice_logp)
    chip = jnp.concatenate(
        [jnp.where(c == 0, slice_logp, other), jnp.where(c == 0, other, slice_logp)], axis=1
    )
    got = [chip] + [send_y(chip, -step) for step in STARTS]
    token_logp = jnp.concatenate(got, axis=1).reshape(-1)

    scores = jnp.sum(jnp.where(wanted, token_logp[None, :], 0.0), axis=1)
    return final_rows, scores.reshape(1, 2 * cap_size)


def solution(mesh):
    in_specs = (
        P("grp", "tp"),
        P(),
        P(),
        P(("grp", "tp"), None),
        P("tp"),
        P("tp", "grp"),
        P("tp", None),
        P("tp", None),
        P("grp", "tp"),
        P("tp"),
        P("tp", "grp"),
        P("tp", "grp"),
        P("grp", "tp"),
        P("tp"),
        P("tp", "grp"),
    )
    out_specs = (P("grp", "tp"), P(("grp", "tp"), None))
    return jax.shard_map(
        per_device, mesh=mesh, in_specs=in_specs, out_specs=out_specs, check_vma=False
    )
```
